768 devices in a mesh: dp: 12 (over z), expert: 32 (over x, y), tensor: 2 (over core).
Axes of the slice: x: 4, y: 8, z: 12, core: 2. Of those that a mesh axis runs over, the one named last changes fastest.
Arguments:
- tokens: bfloat16 [49152, 3584], P(('dp', 'expert')), may hold values from -6 to 6
- routes: int32 [49152, 2], P(('dp', 'expert')), may hold values from 0 to 31, all different within a row; in each aligned block of 128 rows (0 to 127, 128 to 255, ...) at most 9 rows name the same one
- returns: float32 [49152], P(('dp', 'expert')), may hold values from -24 to 24
- router_weight: bfloat16 [3584, 32], replicated, may hold values from -0.09375 to 0.09375
- gate_weight: bfloat16 [32, 3584, 1024], P('expert', None, 'tensor'), may hold values from -0.09375 to 0.09375
- up_weight: bfloat16 [32, 3584, 1024], P('expert', None, 'tensor'), may hold values from -0.09375 to 0.09375
- down_weight: bfloat16 [32, 1024, 3584], P('expert', 'tensor'), may hold values from -0.1875 to 0.1875
- norm_gain: float32 [3584], replicated, may hold values from 0.1 to 1.9
- value_weight: bfloat16 [3584], replicated, may hold values from -0.09375 to 0.09375
Outputs:
- values: float32 [49152], P(('dp', 'expert'))
- router_grad: bfloat16 [3584, 32], replicated
The draws below stay inside these ranges and needn't reach their ends.
Inputs may be any that keep to these rules, and one draw needn't show every extreme that they name: The 2 routes of a token are different experts. Among the tokens of one index of dp and expert no expert is named more than 9 times, and in every draw some such block names some expert exactly 9 times; every expert is named somewhere.
All inputs are finite; a program needn't handle non-finite values.
Results may differ from the reference program's by a relative error of at most 0.017.
Values may be sent and summed in bfloat16 or wider, within the bound.
A program may use at most 64 MiB of HBM per device.

```python
import math
import jax
import jax.numpy as jnp
import numpy as np
from jax import lax

D = 3584
FF = 1024
TOP = 2
TOK_DEV = 128
EXPERTS = 32
CAP = 9
TOKENS = 49152
N_DP = 12
N_EXPERT = 32
N_TENSOR = 2


def shard_levels(key, shape, shards, least, high):
    gain, own = 1.0, jax.random.fold_in(key, 6)
    for dim, shards_of in shards:
        steps = jnp.exp(jax.random.uniform(jax.random.fold_in(own, dim), (shards_of,), jnp.float32, least / len(shards), high / len(shards)))
        gain = gain * jnp.repeat(steps, shape[dim] // shards_of).reshape([-1 if axis == dim else 1 for axis in range(len(shape))])
    return gain


def deal_out(own_key, own, number, rows, amount, top, reach, skew):
    sequence = jax.random.permutation(own_key, amount)
    heavy_load, common = load_shares(amount, rows * top, reach, skew, True), load_shares(amount, rows * top, reach, skew, False)
    places = jnp.arange(amount)

    def named(lengths, turn):
        used = int((lengths > 0).sum())
        fixed = max(1, used // 4)
        moved = fixed + (places - fixed + turn * (used - fixed)) % max(1, amount - fixed)
        return jnp.zeros((amount,), jnp.int32).at[sequence[jnp.where(places < fixed, places, moved)]].set(jnp.asarray(lengths, jnp.int32))

    lengths = jnp.where(number % 4 == 0, named(heavy_load, number // 4), named(common, number - number // 4 - 1))
    mixed = jax.random.permutation(jax.random.fold_in(own, 3), amount)
    source_of, sink = mixed[0:amount // 2 * 2:2], mixed[1:amount // 2 * 2:2]
    slack = jnp.minimum(lengths[source_of] - 1, reach - lengths[sink]) // 2
    slack = jnp.where((source_of == sequence[0]) | (sink == sequence[0]) | (lengths[sink] == 0), 0, jnp.maximum(slack, 0))
    moved = jax.random.randint(jax.random.fold_in(own, 4), (amount // 2,), 0, 1 << 20) % (slack + 1)
    lengths = lengths.at[source_of].add(-moved).at[sink].add(moved)
    items = jnp.searchsorted(jnp.cumsum(lengths), jnp.arange(rows * top), side="right").astype(jnp.int32)
    grid = items.reshape(top, rows).T
    grid = grid[jax.random.permutation(jax.random.fold_in(own, 1), rows)]
    turn = jax.random.randint(jax.random.fold_in(own, 2), (rows, 1), 0, top)
    return jnp.take_along_axis(grid, (jnp.arange(top)[None, :] + turn) % top, axis=1)


def load_shares(number_of, total, most, lean, full):
    portions = [(1 << 20) // math.isqrt(rank ** lean) + 1 for rank in range(1, number_of + 1)]
    largest = most if full else min(most, max(-(-total // number_of), total * portions[0] // sum(portions)))
    least = 1 if total - largest >= number_of - 1 else 0
    holding, rest = [largest] + [least] * (number_of - 1), total - largest - least * (number_of - 1)
    while rest > 0:
        movable = [i for i in range(1, number_of) if holding[i] < largest] or [i for i in range(1, number_of) if holding[i] < most]
        whole, remaining = sum([portions[i] for i in movable]), rest
        for i in movable:
            extra = min(most - holding[i], max(1, remaining * portions[i] // whole), rest)
            holding[i] = holding[i] + extra
            rest = rest - extra
    return np.array(holding)


def gaussian(rng, dims, scale, bound, shards=(), held_as=jnp.bfloat16):
    factor_of = shard_levels(rng, dims, shards, -0.22, 0.18) if shards else 1.0
    result = jax.random.normal(rng, dims, jnp.float32) * scale * factor_of
    return jnp.minimum(jnp.maximum(result, -bound), bound).astype(held_as)


def setup_inputs(seed: int = 0) -> dict:
    keys = jax.random.split(jax.random.key(seed), 10)
    tokens = gaussian(keys[0], (TOKENS, D), 1.0, 6.0, ((0, 384),))
    routes_keys = jax.random.split(jax.random.fold_in(keys[1], 1), TOKENS // TOK_DEV)
    routes_turns = jax.random.permutation(jax.random.fold_in(keys[1], 3), TOKENS // TOK_DEV)
    routes = jax.vmap(lambda own, number: deal_out(jax.random.fold_in(keys[1], 2), own, number, TOK_DEV, EXPERTS, TOP, CAP, 2))(routes_keys, routes_turns).reshape((TOKENS, TOP))
    returns = gaussian(keys[2], (TOKENS,), 4.0, 24.0, ((0, 384),), jnp.float32)
    router_weight = gaussian(keys[3], (D, EXPERTS), D ** -0.5, 0.09375)
    gate_weight = gaussian(keys[4], (EXPERTS, D, FF), D ** -0.5, 0.09375, ((0, 32), (2, 2)))
    up_weight = gaussian(keys[5], (EXPERTS, D, FF), D ** -0.5, 0.09375, ((0, 32), (2, 2)))
    down_weight = gaussian(keys[6], (EXPERTS, FF, D), FF ** -0.5, 0.1875, ((0, 32), (1, 2)))
    norm_gain = jnp.clip(1.0 + 0.18 * jax.random.normal(keys[7], (D,), jnp.float32), 0.1, 1.9)
    value_weight = gaussian(keys[8], (D,), D ** -0.5, 0.09375)
    return dict(tokens=tokens, routes=routes, returns=returns, router_weight=router_weight, gate_weight=gate_weight, up_weight=up_weight, down_weight=down_weight, norm_gain=norm_gain, value_weight=value_weight)


eps = 1e-06
route_scale = 2.5

def rescale(raw):
    return jnp.sign(raw) * (jnp.sqrt(jnp.abs(raw) + 1.0) - 1.0) + 0.001 * raw

def head_and_router(tok_block, route_block, return_block, out_block, router_weight, norm_gain, value_weight):
    logits = jnp.dot(tok_block, router_weight, preferred_element_type=jnp.float32)
    scores = jax.nn.sigmoid(logits)
    chosen = jnp.take_along_axis(scores, route_block, axis=1)
    score_sum = lax.optimization_barrier(jnp.sum(chosen, axis=1, keepdims=True))
    weights = chosen / score_sum
    expert_f = out_block.astype(jnp.float32)
    mixture = lax.optimization_barrier(jnp.sum(weights[:, :, None] * expert_f, axis=1))
    residual = tok_block.astype(jnp.float32) + route_scale * mixture
    inverse = lax.rsqrt(lax.optimization_barrier(jnp.mean(residual * residual, axis=1, keepdims=True)) + eps)
    gained = norm_gain.astype(jnp.float32) * value_weight.astype(jnp.float32)
    values = lax.optimization_barrier(jnp.sum(residual * inverse * gained[None, :], axis=1))
    value_error = values - rescale(return_block)
    direction = gained[None, :] * value_error[:, None]
    grad_resid = inverse * direction - residual * inverse * inverse * inverse * lax.optimization_barrier(jnp.mean(residual * direction, axis=1, keepdims=True))
    grad_weights = route_scale * lax.optimization_barrier(jnp.sum(grad_resid[:, None, :] * expert_f, axis=2))
    centered = grad_weights - lax.optimization_barrier(jnp.sum(weights * grad_weights, axis=1, keepdims=True))
    grad_logits = centered / score_sum * chosen * (1.0 - chosen)
    columns = jnp.arange(router_weight.shape[1], dtype=jnp.int32)
    marks = (route_block[:, :, None] == columns[None, None, :]).astype(jnp.float32)
    dense_grad = lax.optimization_barrier(jnp.sum(marks * grad_logits[:, :, None], axis=1)).astype(jnp.bfloat16)
    return (values, dense_grad)

def reference(tokens, routes, returns, router_weight, gate_weight, up_weight, down_weight, norm_gain, value_weight):
    sources = N_DP * N_EXPERT
    per_source = TOK_DEV * TOP
    routed = routes.reshape(sources, per_source)
    onehot = (routed[:, :, None] == jnp.arange(EXPERTS, dtype=jnp.int32)[None, None, :]).astype(jnp.int32)
    position = lax.optimization_barrier(jnp.sum(jnp.cumsum(onehot, axis=1) * onehot, axis=2)) - 1
    slot_row = jnp.arange(sources, dtype=jnp.int32)[:, None] * CAP + position
    assign_ids = jnp.arange(sources * per_source, dtype=jnp.int32).reshape(sources, per_source)
    table = jnp.full((EXPERTS, sources * CAP), -1, jnp.int32).at[routed, slot_row].set(assign_ids)
    block_ff = FF // N_TENSOR

    def one_expert(expert_id):
        ids = table[expert_id]
        picked = tokens[jnp.maximum(ids, 0) // TOP]
        picked = jnp.where((ids >= 0)[:, None], picked, jnp.zeros_like(picked))
        gate = jnp.dot(picked, gate_weight[expert_id], preferred_element_type=jnp.float32)
        upward = jnp.dot(picked, up_weight[expert_id], preferred_element_type=jnp.float32)
        hidden = (jax.nn.silu(gate) * upward).astype(jnp.bfloat16)
        split_hidden = hidden.reshape(-1, N_TENSOR, block_ff).astype(jnp.float32)
        split_down = down_weight[expert_id].reshape(N_TENSOR, block_ff, D).astype(jnp.float32)
        partials = jnp.einsum('rnf,nfd->nrd', split_hidden, split_down)
        partials = lax.optimization_barrier(partials.astype(jnp.bfloat16)).astype(jnp.float32)
        return lax.optimization_barrier(jnp.sum(partials, axis=0)).astype(jnp.bfloat16)
    expert_all = lax.map(one_expert, jnp.arange(EXPERTS, dtype=jnp.int32))
    gathered = expert_all[routed, slot_row].reshape(sources, TOK_DEV, TOP, D)

    def one_block(pieces):
        tok_block, route_block, return_block, out_block = pieces
        return head_and_router(tok_block, route_block, return_block, out_block, router_weight, norm_gain, value_weight)
    values, dense_grad = lax.map(one_block, (tokens.reshape(sources, TOK_DEV, D), routes.reshape(sources, TOK_DEV, TOP), returns.reshape(sources, TOK_DEV), gathered))
    dense_grad = dense_grad.reshape(TOKENS, EXPERTS)
    router_grad = lax.dot_general(tokens, dense_grad, (((0,), (0,)), ((), ())), preferred_element_type=jnp.float32)
    return (values.reshape(TOKENS), router_grad.astype(jnp.bfloat16))
```

```python
import functools
import jax
import jax.numpy as jnp
from jax import lax
from jax.experimental import pallas as pl
from jax.experimental.pallas import tpu as pltpu
from jax.sharding import PartitionSpec as P

MESH = pl.DeviceIdType.MESH
F32 = jnp.float32
BF16 = jnp.bfloat16
eps = 1e-06
route_scale = 2.5
LANES = 128
EIGHT = 8
TILE = 16


class Plan:
    def __init__(self, mesh, tokens, width, hidden):
        self.nz, self.groups = mesh.shape["dp"], mesh.shape["expert"]
        self.ny = 8 if self.groups >= 32 else 2
        self.nx = self.groups // self.ny
        self.steps = ((0, 4), (3, 5), (2, 6), (1, 7)) if self.ny == 8 else ((0,), (1,))
        self.chunks = len(self.steps)
        self.each = self.groups // self.chunks
        self.tokens, self.width, self.hidden = tokens, width, hidden
        self.half = width // 2
        self.quarter = width // 4
        self.pieces = self.half // LANES
        self.packed = self.quarter + LANES
        self.main = self.each * EIGHT
        self.rows = self.main + max(TILE, self.each)


def expert_kernel(
    plan,
    tok_ref,
    routes_ref,
    returns_ref,
    router_ref,
    gate_hbm,
    up_hbm,
    down_hbm,
    gain_ref,
    head_ref,
    values_ref,
    grad_ref,
    wg,
    wu,
    wd,
    out,
    arr,
    oth,
    xs,
    pxo,
    pxi,
    ret,
    back,
    qs,
    mix,
    nine,
    tmp9,
    wide9,
    chosen_ref,
    sums_out,
    sums_in,
    dlo,
    dli,
    zb,
    row9,
    agb,
    w_sem,
    out_s,
    out_r,
    fwd_s,
    fwd_r,
    px_s,
    px_r,
    ret_s,
    ret_r,
    sum_s,
    sum_r,
    dl_s,
    dl_r,
    z_s,
    z_r,
    ag_s,
    ag_r,
    agx_s,
    agx_r,
):
    T, D, H, Q4 = plan.tokens, plan.width, plan.half, plan.quarter
    NZ, NE, NX, NY = plan.nz, plan.groups, plan.nx, plan.ny
    NC, CD, MAIN, XR = plan.chunks, plan.each, plan.main, plan.rows
    z = lax.axis_index("dp")
    me = lax.axis_index("expert")
    c = lax.axis_index("tensor")
    other = 1 - c
    mx, my = lax.div(me, NY), lax.rem(me, NY)

    def hops(j, i):
        dx, b = lax.rem(i, NX), lax.div(i, NX)
        first = plan.steps[j][0]
        return dx, (first + b * (plan.steps[j][1] - first) if len(plan.steps[j]) > 1 else first)

    def ahead(j, i):
        dx, dy = hops(j, i)
        return lax.rem(mx + dx, NX) * NY + lax.rem(my + dy, NY)

    def behind(j, i):
        dx, dy = hops(j, i)
        return lax.rem(mx - dx + NX, NX) * NY + lax.rem(my - dy + NY, NY)

    def partners(j, body):
        def run(i, carry):
            body(jnp.int32(j * CD) + i, i)
            return carry

        lax.fori_loop(1 if j == 0 else 0, CD, run, 0)

    loads = [
        pltpu.make_async_copy(gate_hbm.at[0], wg, w_sem.at[0]),
        pltpu.make_async_copy(up_hbm.at[0], wu, w_sem.at[1]),
        pltpu.make_async_copy(down_hbm.at[0, :, pl.ds(0, H)], wd.at[0], w_sem.at[2]),
        pltpu.make_async_copy(down_hbm.at[0, :, pl.ds(H, H)], wd.at[1], w_sem.at[3]),
    ]
    for load in loads:
        load.start()

    barrier = pltpu.get_barrier_semaphore()
    for j in range(NC):
        partners(
            j,
            lambda d, i, j=j: pl.semaphore_signal(
                barrier, inc=1, device_id=(z, ahead(j, i), c), device_id_type=MESH
            ),
        )

    def greet(dz, carry):
        pl.semaphore_signal(
            barrier, inc=1, device_id=(lax.rem(z + dz, NZ), me, c), device_id_type=MESH
        )
        return carry

    lax.fori_loop(1, NZ, greet, 0)
    pl.semaphore_signal(barrier, inc=1, device_id=(z, me, other), device_id_type=MESH)

    def out_copy(j, d, i):
        return pltpu.make_async_remote_copy(
            out.at[d], arr.at[d], out_s.at[d], out_r.at[d], (z, ahead(j, i), c), MESH
        )

    def fwd_copy(d):
        return pltpu.make_async_remote_copy(
            arr.at[d], oth.at[d], fwd_s.at[d], fwd_r.at[d], (z, me, other), MESH
        )

    def px_copy(j):
        part = pl.ds(j * CD, CD)
        return pltpu.make_async_remote_copy(
            pxo.at[part], pxi.at[part], px_s.at[j], px_r.at[j], (z, me, other), MESH
        )

    def ret_copy(j, d, i):
        return pltpu.make_async_remote_copy(
            ret.at[d], back.at[d], ret_s.at[d], ret_r.at[d], (z, behind(j, i), c), MESH
        )

    def dl_copy(j, d, i):
        return pltpu.make_async_remote_copy(
            dlo.at[j], dli.at[d], dl_s.at[d], dl_r.at[d], (z, ahead(j, i), c), MESH
        )

    lane = lax.broadcasted_iota(jnp.int32, (1, LANES), 1)
    lane_i = jnp.where(lane < MAIN, lax.shift_right_logical(lane, 3), lane - MAIN)
    lane_slot = jnp.where(lane < MAIN, jnp.bitwise_and(lane, 7) + 1, EIGHT + 1)
    lane_slot = jnp.where(lane < MAIN + CD, lane_slot, -1).astype(F32)
    x_bits = NX.bit_length() - 1
    lane_dx = jnp.bitwise_and(lane_i, NX - 1)
    lane_b = lax.shift_right_logical(lane_i, x_bits)

    def lane_expert(j):
        dy = jnp.full((1, LANES), plan.steps[j][0], jnp.int32)
        for b in range(1, len(plan.steps[j])):
            dy = jnp.where(lane_b == b, plan.steps[j][b], dy)
        ex = jnp.bitwise_and(mx + lane_dx, NX - 1)
        ey = jnp.bitwise_and(my + dy, NY - 1)
        return ex * NY + ey

    def pack(dst, j, rows):
        part = pl.ds(j * CD, CD)
        first = rows[0:MAIN, 0:Q4].reshape(CD, EIGHT, Q4)
        second = rows[0:MAIN, Q4:H].reshape(CD, EIGHT, Q4)
        dst[part, :, 0:Q4] = jnp.concatenate([first, second], axis=1).astype(BF16)
        for q in range(plan.pieces):
            nine[pl.ds(q, CD, stride=TILE), :] = rows[MAIN : MAIN + CD, q * LANES : (q + 1) * LANES]
        dst[part, :, Q4:] = nine[...].reshape(CD, TILE, LANES).astype(BF16)

    def unpack(src, j, put):
        part = pl.ds(j * CD, CD)
        both = src[part, :, 0:Q4].astype(F32)
        put(0, MAIN, 0, Q4, both[:, 0:EIGHT].reshape(MAIN, Q4).astype(BF16))
        put(0, MAIN, Q4, Q4, both[:, EIGHT:TILE].reshape(MAIN, Q4).astype(BF16))
        tmp9[...] = src[part, :, Q4:].astype(F32).reshape(CD * TILE, LANES)
        last = jnp.concatenate(
            [tmp9[pl.ds(q, CD, stride=TILE), :] for q in range(plan.pieces)], axis=1
        )
        last = jnp.concatenate([last, jnp.zeros((XR - MAIN - CD, H), F32)], axis=0)
        put(MAIN, XR - MAIN, 0, H, last.astype(BF16))

    expert_of_row = lax.broadcasted_iota(jnp.int32, (LANES, T), 0)
    marks = [
        jnp.transpose((expert_of_row == routes_ref[k : k + 1, :]).astype(F32)) for k in range(2)
    ]
    earlier = (
        lax.broadcasted_iota(jnp.int32, (T, T), 0) > lax.broadcasted_iota(jnp.int32, (T, T), 1)
    ).astype(BF16)
    cum = jnp.dot(earlier, (marks[0] + marks[1]).astype(BF16), preferred_element_type=F32)
    key = jnp.concatenate([marks[0] * (cum + 1.0), marks[1] * (cum + 1.0)], axis=0).astype(BF16)
    nine[...] = jnp.zeros_like(nine)

    columns = pl.ds(pl.multiple_of(c * H, LANES), H)
    for j in range(NC):
        spread = (
            lax.broadcasted_iota(jnp.int32, (LANES, LANES), 0) == lane_expert(j)
        ).astype(BF16)
        named = jnp.dot(key, spread, preferred_element_type=F32)
        place = (named == lane_slot).astype(F32)
        qs[j] = place.astype(BF16)
        pick = jnp.transpose(place[0:T] + place[T : 2 * T])[0:XR].astype(BF16)
        rows = jnp.dot(pick, tok_ref[:, columns], preferred_element_type=F32)
        pack(out, j, rows)
        if j == 0:
            pl.semaphore_wait(barrier, NE - 1 + NZ - 1 + 1)
            arr[0] = out[0]
            fwd_copy(0).start()
        partners(j, lambda d, i, j=j: out_copy(j, d, i).start())

    logits = lax.dot_general(
        tok_ref[...], router_ref[...], (((1,), (1,)), ((), ())), preferred_element_type=F32
    )
    scores = jax.nn.sigmoid(logits)
    for k in range(2):
        chosen = jnp.sum(marks[k][:, 0:NE] * scores, axis=1, keepdims=True)
        chosen_ref[k] = jnp.broadcast_to(chosen, (T, LANES))

    for load in loads:
        load.wait()

    for j in range(NC):

        def arrive(d, i, j=j):
            out_copy(j, d, i).wait_recv()
            fwd_copy(d).start()

        partners(j, arrive)

        def put_own(r, n, col, m, v, j=j):
            xs[j, c, r : r + n, col : col + m] = v

        def put_other(r, n, col, m, v, j=j):
            xs[j, other, r : r + n, col : col + m] = v

        unpack(arr, j, put_own)

        def forwarded(i, carry, j=j):
            fwd_copy(jnp.int32(j * CD) + i).wait_recv()
            return carry

        lax.fori_loop(0, CD, forwarded, 0)
        unpack(oth, j, put_other)
        gate = jnp.dot(xs[j, 0], wg[0:H, :], preferred_element_type=F32)
        gate = gate + jnp.dot(xs[j, 1], wg[H:D, :], preferred_element_type=F32)
        upward = jnp.dot(xs[j, 0], wu[0:H, :], preferred_element_type=F32)
        upward = upward + jnp.dot(xs[j, 1], wu[H:D, :], preferred_element_type=F32)
        hidden = (gate / (1.0 + jnp.exp(-gate)) * upward).astype(BF16)
        pack(pxo, j, jnp.dot(hidden, wd[other], preferred_element_type=F32))
        px_copy(j).start()
        pack(ret, j, jnp.dot(hidden, wd[c], preferred_element_type=F32))
        px_copy(j).wait_recv()
        part = pl.ds(j * CD, CD)
        ret[part] = (ret[part].astype(F32) + pxi[part].astype(F32)).astype(BF16)
        if j == 0:
            back[0] = ret[0]
        partners(j, lambda d, i, j=j: ret_copy(j, d, i).start())

    for j in range(NC):
        partners(j, lambda d, i, j=j: ret_copy(j, d, i).wait_recv())

        pieces = {}

        def keep(r, n, col, m, v, pieces=pieces):
            pieces[(r, col)] = v

        unpack(back, j, keep)
        low = qs[j][:, 0:MAIN]
        high = qs[j][:, MAIN:XR]
        for col in (0, Q4):
            term = jnp.dot(low, pieces[(0, col)], preferred_element_type=F32)
            term = term + jnp.dot(
                high, pieces[(MAIN, 0)][:, col : col + Q4], preferred_element_type=F32
            )
            if j == 0:
                mix[:, col : col + Q4] = term
            else:
                mix[:, col : col + Q4] += term

    block = min(32, T)
    for b in range(T // block):
        low, high = b * block, (b + 1) * block
        first, second = chosen_ref[0, low:high], chosen_ref[1, low:high]
        total = first + second
        w0, w1 = first / total, second / total
        acc = [jnp.zeros((block, LANES), F32) for _ in range(6)]
        for q in range(plan.pieces):
            at = pl.ds(pl.multiple_of(c * H + q * LANES, LANES), LANES)
            gained = gain_ref[:, at] * head_ref[:, at].astype(F32)
            o0 = mix[low:high, q * LANES : (q + 1) * LANES]
            o1 = mix[T + low : T + high, q * LANES : (q + 1) * LANES]
            residual = tok_ref[low:high, at].astype(F32) + route_scale * (w0 * o0 + w1 * o1)
            terms = (
                residual * residual,
                residual * gained,
                residual * o0,
                residual * o1,
                gained * o0,
                gained * o1,
            )
            acc = [a + term for a, term in zip(acc, terms)]
        line = jnp.zeros((block, LANES), F32)
        for n, a in enumerate(acc):
            line = jnp.where(lane == n, jnp.sum(a, axis=1, keepdims=True), line)
        sums_out[low:high, :] = line

    sums_copy = pltpu.make_async_remote_copy(
        sums_out, sums_in, sum_s, sum_r, (z, me, other), MESH
    )
    sums_copy.start()
    raw = jnp.transpose(jnp.broadcast_to(returns_ref[...], (LANES, T)))[:, 0:1]
    sign = jnp.where(raw > 0.0, 1.0, jnp.where(raw < 0.0, -1.0, 0.0))
    target = sign * (jnp.sqrt(jnp.abs(raw) + 1.0) - 1.0) + 0.001 * raw
    first, second = chosen_ref[0][:, 0:1], chosen_ref[1][:, 0:1]
    score_sum = first + second
    w0, w1 = first / score_sum, second / score_sum
    sums_copy.wait_recv()
    sums = sums_out[...] + sums_in[...]
    rr, rg, ro0, ro1, go0, go1 = [sums[:, n : n + 1] for n in range(6)]
    inverse = lax.rsqrt(rr * (1.0 / D) + eps)
    values = rg * inverse
    values_ref[...] = jnp.transpose(jnp.broadcast_to(values, (T, LANES)))[0:1, :]
    error = values - target
    pull = inverse * inverse * inverse * (error * rg * (1.0 / D))
    gw0 = route_scale * (inverse * error * go0 - pull * ro0)
    gw1 = route_scale * (inverse * error * go1 - pull * ro1)
    centre = w0 * gw0 + w1 * gw1
    gl0 = (gw0 - centre) / score_sum * first * (1.0 - first)
    gl1 = (gw1 - centre) / score_sum * second * (1.0 - second)
    both = jnp.concatenate([gl0, gl1], axis=0).astype(BF16).astype(F32)

    for j in range(NC):
        dlo[j] = jnp.sum(qs[j].astype(F32) * both, axis=0, keepdims=True)
        if j == 0:
            dli[0] = dlo[0]
        partners(j, lambda d, i, j=j: dl_copy(j, d, i).start())

    grad = jnp.zeros((1, H), F32)
    for j in range(NC):
        partners(j, lambda d, i, j=j: dl_copy(j, d, i).wait_recv())
        got = dli[j * CD : (j + 1) * CD]
        mine = lax.broadcasted_iota(jnp.int32, (CD, 1, LANES), 0) == lane_i.reshape(1, 1, LANES)
        line = jnp.sum(jnp.where(mine, got, 0.0), axis=0)
        line = jnp.broadcast_to(line, (TILE, LANES)).astype(BF16)[:, 0:XR]
        grad = grad + jnp.dot(line, xs[j, c], preferred_element_type=F32)[0:1]

    zb[z] = grad

    def z_copy(dz):
        return pltpu.make_async_remote_copy(
            zb.at[z], zb.at[z], z_s.at[dz], z_r.at[z], (lax.rem(z + dz, NZ), me, c), MESH
        )

    def z_from(dz):
        source = lax.rem(z - dz + NZ, NZ)
        return pltpu.make_async_remote_copy(
            zb.at[source], zb.at[source], z_s.at[dz], z_r.at[source], (source, me, c), MESH
        )

    def z_start(dz, carry):
        z_copy(dz).start()
        return carry

    def z_wait(dz, carry):
        z_from(dz).wait_recv()
        return carry

    lax.fori_loop(1, NZ, z_start, 0)
    lax.fori_loop(1, NZ, z_wait, 0)
    grad = zb[0]
    for source in range(1, NZ):
        grad = grad + zb[source]

    row9[...] = jnp.zeros_like(row9)
    for q in range(plan.pieces):
        row9[q : q + 1, :] = grad[:, q * LANES : (q + 1) * LANES]
    agb[c, me] = row9[...].astype(BF16)

    def ag_copy(j, d, i):
        return pltpu.make_async_remote_copy(
            agb.at[c, me], agb.at[c, me], ag_s.at[d], ag_r.at[d], (z, ahead(j, i), c), MESH
        )

    def ag_from(j, d, i):
        source = behind(j, i)
        return pltpu.make_async_remote_copy(
            agb.at[c, source], agb.at[c, source], ag_s.at[d], ag_r.at[d], (z, source, c), MESH
        )

    for j in range(NC):
        partners(j, lambda d, i, j=j: ag_copy(j, d, i).start())
    for j in range(NC):
        partners(j, lambda d, i, j=j: ag_from(j, d, i).wait_recv())
    agx = pltpu.make_async_remote_copy(
        agb.at[c], agb.at[c], agx_s, agx_r, (z, me, other), MESH
    )
    agx.start()

    for j in range(NC):
        px_copy(j).wait_send()

        def left(d, i, j=j):
            out_copy(j, d, i).wait_send()
            ret_copy(j, d, i).wait_send()
            dl_copy(j, d, i).wait_send()
            ag_copy(j, d, i).wait_send()

        partners(j, left)

    def left_chip(d, carry):
        fwd_copy(d).wait_send()
        return carry

    def left_plane(dz, carry):
        z_copy(dz).wait_send()
        return carry

    lax.fori_loop(0, NE, left_chip, 0)
    lax.fori_loop(1, NZ, left_plane, 0)
    sums_copy.wait_send()

    def write(part):
        wide9[...] = agb[part].astype(F32).reshape(NE * TILE, LANES)
        for q in range(plan.pieces):
            at = pl.ds(pl.multiple_of(part * H + q * LANES, LANES), LANES)
            grad_ref[:, at] = wide9[pl.ds(q, NE, stride=TILE), :].astype(BF16)

    write(c)
    agx.wait()
    write(other)


def on_device(
    mesh,
    tokens,
    routes,
    returns,
    router_weight,
    gate_weight,
    up_weight,
    down_weight,
    norm_gain,
    value_weight,
):
    count, width = tokens.shape
    hidden = gate_weight.shape[2]
    plan = Plan(mesh, count, width, hidden)
    NE, NC, H = plan.groups, plan.chunks, plan.half
    packed = (NE, TILE, plan.packed)
    vmem, dma = pltpu.VMEM, pltpu.SemaphoreType.DMA
    in_vmem = pl.BlockSpec(memory_space=pltpu.VMEM)
    in_place = pl.BlockSpec(memory_space=pl.ANY)
    values, grad = pl.pallas_call(
        functools.partial(expert_kernel, plan),
        out_shape=(
            jax.ShapeDtypeStruct((1, count), F32),
            jax.ShapeDtypeStruct((NE, width), BF16),
        ),
        in_specs=[in_vmem] * 4 + [in_place] * 3 + [in_vmem] * 2,
        out_specs=(in_vmem, in_vmem),
        scratch_shapes=[
            vmem((width, hidden), BF16),
            vmem((width, hidden), BF16),
            vmem((2, hidden, H), BF16),
            vmem(packed, BF16),
            vmem(packed, BF16),
            vmem(packed, BF16),
            vmem((NC, 2, plan.rows, H), BF16),
            vmem(packed, BF16),
            vmem(packed, BF16),
            vmem(packed, BF16),
            vmem(packed, BF16),
            vmem((NC, 2 * count, LANES), BF16),
            vmem((2 * count, H), F32),
            vmem((plan.each * TILE, LANES), F32),
            vmem((plan.each * TILE, LANES), F32),
            vmem((NE * TILE, LANES), F32),
            vmem((2, count, LANES), F32),
            vmem((count, LANES), F32),
            vmem((count, LANES), F32),
            vmem((NC, 1, LANES), F32),
            vmem((NE, 1, LANES), F32),
            vmem((plan.nz, 1, H), F32),
            vmem((TILE, LANES), F32),
            vmem((2, NE, TILE, LANES), BF16),
            dma((4,)),
            dma((NE,)),
            dma((NE,)),
            dma((NE,)),
            dma((NE,)),
            dma((NC,)),
            dma((NC,)),
            dma((NE,)),
            dma((NE,)),
            dma,
            dma,
            dma((NE,)),
            dma((NE,)),
            dma((plan.nz,)),
            dma((plan.nz,)),
            dma((NE,)),
            dma((NE,)),
            dma,
            dma,
        ],
        compiler_params=pltpu.CompilerParams(
            collective_id=0, has_side_effects=True, vmem_limit_bytes=50 * 1024 * 1024
        ),
        cost_estimate=pl.CostEstimate(
            flops=6 * NE * 9 * width * hidden,
            bytes_accessed=6 * width * hidden,
            transcendentals=NE * 9 * hidden,
        ),
    )(
        tokens,
        routes.T,
        returns.reshape(1, count),
        router_weight.T,
        gate_weight,
        up_weight,
        down_weight,
        norm_gain.reshape(1, width),
        value_weight.reshape(1, width),
    )
    return values.reshape(count), grad.T


def solution(mesh):
    return jax.shard_map(
        functools.partial(on_device, mesh),
        mesh=mesh,
        in_specs=(
            P(("dp", "expert"), None),
            P(("dp", "expert"), None),
            P(("dp", "expert")),
            P(),
            P("expert", None, "tensor"),
            P("expert", None, "tensor"),
            P("expert", "tensor", None),
            P(),
            P(),
        ),
        out_specs=(P(("dp", "expert")), P()),
        check_vma=False,
    )
```

```python
import functools
import jax
import jax.numpy as jnp
from jax import lax
from jax.experimental import pallas as pl
from jax.experimental.pallas import tpu as pltpu
from jax.sharding import PartitionSpec as P

MESH = pl.DeviceIdType.MESH
F32 = jnp.float32
BF16 = jnp.bfloat16
eps = 1e-06
route_scale = 2.5
LANES = 128
EIGHT = 8
TILE = 16


class Plan:
    def __init__(self, mesh, tokens, width, hidden):
        self.nz, self.groups = mesh.shape["dp"], mesh.shape["expert"]
        self.ny = 8 if self.groups >= 32 else 2
        self.nx = self.groups // self.ny
        self.steps = ((0, 4), (2, 6), (3, 5), (1, 7)) if self.ny == 8 else ((0,), (1,))
        self.chunks = len(self.steps)
        self.home = [one[0] for one in self.steps].index(0)
        self.each = self.groups // self.chunks
        self.tokens, self.width, self.hidden = tokens, width, hidden
        self.half = width // 2
        self.quarter = width // 4
        self.pieces = self.half // LANES
        self.packed = self.quarter + LANES
        self.main = self.each * EIGHT
        self.rows = self.main + max(TILE, self.each)


def expert_kernel(
    plan,
    tok_hbm,
    routes_hbm,
    returns_hbm,
    router_hbm,
    gate_hbm,
    up_hbm,
    down_hbm,
    gain_hbm,
    head_hbm,
    values_ref,
    grad_ref,
    tok_ref,
    routes_ref,
    returns_ref,
    router_ref,
    gain_ref,
    head_ref,
    gained_ref,
    wg,
    wu,
    wd,
    out,
    arr,
    oth,
    xs,
    pxo,
    pxi,
    ret,
    back,
    qs,
    answer,
    mix,
    nine,
    tmp9,
    wide9,
    chosen_ref,
    sums_out,
    sums_in,
    dlo,
    dli,
    zb,
    row9,
    agb,
    values_out,
    grad_out,
    w_sem,
    out_s,
    out_r,
    fwd_s,
    fwd_r,
    px_s,
    px_r,
    ret_s,
    ret_r,
    sum_s,
    sum_r,
    dl_s,
    dl_r,
    z_s,
    z_r,
    ag_s,
    ag_r,
    agx_s,
    agx_r,
):
    T, D, H, Q4 = plan.tokens, plan.width, plan.half, plan.quarter
    NZ, NE, NX, NY = plan.nz, plan.groups, plan.nx, plan.ny
    NC, CD, MAIN, XR = plan.chunks, plan.each, plan.main, plan.rows
    z = lax.axis_index("dp")
    me = lax.axis_index("expert")
    c = lax.axis_index("tensor")
    other = 1 - c
    own = plan.home * plan.each
    mx, my = lax.div(me, NY), lax.rem(me, NY)

    def hops(j, i):
        dx, b = lax.rem(i, NX), lax.div(i, NX)
        first = plan.steps[j][0]
        return dx, (first + b * (plan.steps[j][1] - first) if len(plan.steps[j]) > 1 else first)

    def ahead(j, i):
        dx, dy = hops(j, i)
        return lax.rem(mx + dx, NX) * NY + lax.rem(my + dy, NY)

    def behind(j, i):
        dx, dy = hops(j, i)
        return lax.rem(mx - dx + NX, NX) * NY + lax.rem(my - dy + NY, NY)

    def partners(j, body):
        def run(i, carry):
            body(jnp.int32(j * CD) + i, i)
            return carry

        lax.fori_loop(1 if j == plan.home else 0, CD, run, 0)

    def load(source, target, n):
        return pltpu.make_async_copy(source, target, w_sem.at[n])

    route_load = load(routes_hbm, routes_ref, 0)
    route_load.start()
    token_load = load(tok_hbm, tok_ref, 1)
    token_load.start()

    barrier = pltpu.get_barrier_semaphore()
    for j in range(NC):
        partners(
            j,
            lambda d, i, j=j: pl.semaphore_signal(
                barrier, inc=1, device_id=(z, ahead(j, i), c), device_id_type=MESH
            ),
        )

    def greet(dz, carry):
        pl.semaphore_signal(
            barrier, inc=1, device_id=(lax.rem(z + dz, NZ), me, c), device_id_type=MESH
        )
        return carry

    lax.fori_loop(1, NZ, greet, 0)
    pl.semaphore_signal(barrier, inc=1, device_id=(z, me, other), device_id_type=MESH)

    small_loads = [
        load(router_hbm, router_ref, 2),
        load(returns_hbm, returns_ref, 3),
        load(gain_hbm, gain_ref, 4),
        load(head_hbm, head_ref, 5),
    ]
    weight_loads = [
        load(gate_hbm.at[0], wg, 6),
        load(up_hbm.at[0], wu, 7),
        load(down_hbm.at[0, :, pl.ds(0, H)], wd.at[0], 8),
        load(down_hbm.at[0, :, pl.ds(H, H)], wd.at[1], 9),
    ]
    for one in small_loads + weight_loads:
        one.start()

    def out_copy(j, d, i):
        return pltpu.make_async_remote_copy(
            out.at[d], arr.at[d], out_s.at[d], out_r.at[d], (z, ahead(j, i), c), MESH
        )

    def fwd_copy(d):
        return pltpu.make_async_remote_copy(
            arr.at[d], oth.at[d], fwd_s.at[d], fwd_r.at[d], (z, me, other), MESH
        )

    def px_copy(j):
        part = pl.ds(j * CD, CD)
        return pltpu.make_async_remote_copy(
            pxo.at[part], pxi.at[part], px_s.at[j], px_r.at[j], (z, me, other), MESH
        )

    def ret_copy(j, d, i):
        return pltpu.make_async_remote_copy(
            ret.at[d], back.at[d], ret_s.at[d], ret_r.at[d], (z, behind(j, i), c), MESH
        )

    def dl_copy(j, d, i):
        return pltpu.make_async_remote_copy(
            dlo.at[j], dli.at[d], dl_s.at[d], dl_r.at[d], (z, ahead(j, i), c), MESH
        )

    def partner_of(l):
        return jnp.where(l < MAIN, lax.shift_right_logical(l, 3), l - MAIN)

    def slot_of(l):
        slot = jnp.where(l < MAIN, jnp.bitwise_and(l, 7) + 1, EIGHT + 1)
        return jnp.where(l < MAIN + CD, slot, -1).astype(F32)

    def expert_of(l, j):
        i = partner_of(l)
        b = lax.shift_right_logical(i, NX.bit_length() - 1)
        dy = jnp.full(l.shape, plan.steps[j][0], jnp.int32)
        for n in range(1, len(plan.steps[j])):
            dy = jnp.where(b == n, plan.steps[j][n], dy)
        ex = jnp.bitwise_and(mx + jnp.bitwise_and(i, NX - 1), NX - 1)
        return ex * NY + jnp.bitwise_and(my + dy, NY - 1)

    lane = lax.broadcasted_iota(jnp.int32, (1, LANES), 1)
    lane_i, lane_slot = partner_of(lane), slot_of(lane)

    def pack(dst, j, rows):
        part = pl.ds(j * CD, CD)
        first = rows[0:MAIN, 0:Q4].reshape(CD, EIGHT, Q4)
        second = rows[0:MAIN, Q4:H].reshape(CD, EIGHT, Q4)
        dst[part, :, 0:Q4] = jnp.concatenate([first, second], axis=1).astype(BF16)
        for q in range(plan.pieces):
            nine[pl.ds(q, CD, stride=TILE), :] = rows[MAIN : MAIN + CD, q * LANES : (q + 1) * LANES]
        dst[part, :, Q4:] = nine[...].reshape(CD, TILE, LANES).astype(BF16)

    def unpack(src, j, put):
        part = pl.ds(j * CD, CD)
        both = src[part, :, 0:Q4].astype(F32)
        put(0, MAIN, 0, Q4, both[:, 0:EIGHT].reshape(MAIN, Q4).astype(BF16))
        put(0, MAIN, Q4, Q4, both[:, EIGHT:TILE].reshape(MAIN, Q4).astype(BF16))
        tmp9[...] = src[part, :, Q4:].astype(F32).reshape(CD * TILE, LANES)
        last = jnp.concatenate(
            [tmp9[pl.ds(q, CD, stride=TILE), :] for q in range(plan.pieces)], axis=1
        )
        last = jnp.concatenate([last, jnp.zeros((XR - MAIN - CD, H), F32)], axis=0)
        put(MAIN, XR - MAIN, 0, H, last.astype(BF16))

    nine[...] = jnp.zeros_like(nine)
    expert_row = lax.broadcasted_iota(jnp.int32, (NE, T), 0)
    before = (
        lax.broadcasted_iota(jnp.int32, (T, T), 0) < lax.broadcasted_iota(jnp.int32, (T, T), 1)
    ).astype(BF16)
    slot_row = lax.broadcasted_iota(jnp.int32, (XR, NE), 0)
    expert_column = lax.broadcasted_iota(jnp.int32, (XR, NE), 1)
    row_slot = slot_of(lax.broadcasted_iota(jnp.int32, (XR, T), 0))
    spreads = [(expert_column == expert_of(slot_row, j)).astype(BF16) for j in range(NC)]
    route_load.wait()
    named = (expert_row == routes_ref[0:1, :]) | (expert_row == routes_ref[1:2, :])
    named = named.astype(F32)
    earlier = jnp.dot(named.astype(BF16), before, preferred_element_type=F32)
    key = (named * (earlier + 1.0)).astype(BF16)
    picks = []
    for j in range(NC):
        spread = jnp.dot(spreads[j], key, preferred_element_type=F32)
        picks.append((spread == row_slot).astype(BF16))

    columns = pl.ds(pl.multiple_of(c * H, LANES), H)
    token_load.wait()
    for j in range(NC):
        pack(out, j, jnp.dot(picks[j], tok_ref[:, columns], preferred_element_type=F32))
        if j == 0:
            pl.semaphore_wait(barrier, NE - 1 + NZ - 1 + 1)
        partners(j, lambda d, i, j=j: out_copy(j, d, i).start())
        if j == plan.home:
            arr[own] = out[own]
            fwd_copy(own).start()

    marks = [
        jnp.transpose(
            (
                lax.broadcasted_iota(jnp.int32, (LANES, T), 0) == routes_ref[k : k + 1, :]
            ).astype(F32)
        )
        for k in range(2)
    ]
    after = (
        lax.broadcasted_iota(jnp.int32, (T, T), 0) > lax.broadcasted_iota(jnp.int32, (T, T), 1)
    ).astype(BF16)
    cum = jnp.dot(after, (marks[0] + marks[1]).astype(BF16), preferred_element_type=F32)
    key = jnp.concatenate([marks[0] * (cum + 1.0), marks[1] * (cum + 1.0)], axis=0).astype(BF16)
    for j in range(NC):
        spread = (lax.broadcasted_iota(jnp.int32, (LANES, LANES), 0) == expert_of(lane, j)).astype(
            BF16
        )
        spread = jnp.dot(key, spread, preferred_element_type=F32)
        qs[j] = (spread == lane_slot).astype(F32).astype(BF16)

    for one in small_loads:
        one.wait()
    for n in range(0, D, 2 * LANES):
        gained = gain_ref[n : n + 2 * LANES] * head_ref[n : n + 2 * LANES].astype(F32)
        gained_ref[:, n : n + 2 * LANES] = gained.reshape(1, 2 * LANES)
    logits = lax.dot_general(
        tok_ref[...], router_ref[...], (((1,), (1,)), ((), ())), preferred_element_type=F32
    )
    scores = jax.nn.sigmoid(logits)
    for k in range(2):
        chosen = jnp.sum(marks[k][:, 0:NE] * scores, axis=1, keepdims=True)
        chosen_ref[k] = jnp.broadcast_to(chosen, (T, LANES))

    for one in weight_loads:
        one.wait()

    for j in range(NC):

        def arrive(d, i, j=j):
            out_copy(j, d, i).wait_recv()
            fwd_copy(d).start()

        partners(j, arrive)

        def put_own(r, n, col, m, v, j=j):
            xs[j, c, r : r + n, col : col + m] = v

        def put_other(r, n, col, m, v, j=j):
            xs[j, other, r : r + n, col : col + m] = v

        unpack(arr, j, put_own)

        def forwarded(i, carry, j=j):
            fwd_copy(jnp.int32(j * CD) + i).wait_recv()
            return carry

        lax.fori_loop(0, CD, forwarded, 0)
        unpack(oth, j, put_other)
        gate = jnp.dot(xs[j, 0], wg[0:H, :], preferred_element_type=F32)
        gate = gate + jnp.dot(xs[j, 1], wg[H:D, :], preferred_element_type=F32)
        upward = jnp.dot(xs[j, 0], wu[0:H, :], preferred_element_type=F32)
        upward = upward + jnp.dot(xs[j, 1], wu[H:D, :], preferred_element_type=F32)
        hidden = (gate / (1.0 + jnp.exp(-gate)) * upward).astype(BF16)
        pack(pxo, j, jnp.dot(hidden, wd[other], preferred_element_type=F32))
        px_copy(j).start()
        pack(ret, j, jnp.dot(hidden, wd[c], preferred_element_type=F32))
        px_copy(j).wait_recv()
        part = pl.ds(j * CD, CD)
        ret[part] = (ret[part].astype(F32) + pxi[part].astype(F32)).astype(BF16)
        if j == plan.home:
            back[own] = ret[own]
        partners(j, lambda d, i, j=j: ret_copy(j, d, i).start())

    for j in range(NC):
        px_copy(j).wait_send()
        partners(j, lambda d, i, j=j: out_copy(j, d, i).wait_send())

    def left_chip(d, carry):
        fwd_copy(d).wait_send()
        return carry

    lax.fori_loop(0, NE, left_chip, 0)

    def put_answer(r, n, col, m, v):
        answer[r : r + n, col : col + m] = v

    for j in range(NC):
        partners(j, lambda d, i, j=j: ret_copy(j, d, i).wait_recv())
        unpack(back, j, put_answer)
        term = jnp.dot(qs[j][:, 0:XR], answer[...], preferred_element_type=F32)
        if j == 0:
            mix[...] = term
        else:
            mix[...] += term

    block = min(32, T)
    for b in range(T // block):
        low, high = b * block, (b + 1) * block
        first, second = chosen_ref[0, low:high], chosen_ref[1, low:high]
        total = first + second
        w0, w1 = first / total, second / total
        acc = [jnp.zeros((block, LANES), F32) for _ in range(6)]
        for q in range(plan.pieces):
            at = pl.ds(pl.multiple_of(c * H + q * LANES, LANES), LANES)
            gained = gained_ref[:, at]
            o0 = mix[low:high, q * LANES : (q + 1) * LANES]
            o1 = mix[T + low : T + high, q * LANES : (q + 1) * LANES]
            residual = tok_ref[low:high, at].astype(F32) + route_scale * (w0 * o0 + w1 * o1)
            terms = (
                residual * residual,
                residual * gained,
                residual * o0,
                residual * o1,
                gained * o0,
                gained * o1,
            )
            acc = [a + term for a, term in zip(acc, terms)]
        line = jnp.zeros((block, LANES), F32)
        for n, a in enumerate(acc):
            line = jnp.where(lane == n, jnp.sum(a, axis=1, keepdims=True), line)
        sums_out[low:high, :] = line

    sums_copy = pltpu.make_async_remote_copy(
        sums_out, sums_in, sum_s, sum_r, (z, me, other), MESH
    )
    sums_copy.start()
    raw = jnp.transpose(jnp.broadcast_to(returns_ref[...], (LANES, T)))[:, 0:1]
    sign = jnp.where(raw > 0.0, 1.0, jnp.where(raw < 0.0, -1.0, 0.0))
    target = sign * (jnp.sqrt(jnp.abs(raw) + 1.0) - 1.0) + 0.001 * raw
    first, second = chosen_ref[0][:, 0:1], chosen_ref[1][:, 0:1]
    score_sum = first + second
    w0, w1 = first / score_sum, second / score_sum
    sums_copy.wait_recv()
    sums = sums_out[...] + sums_in[...]
    rr, rg, ro0, ro1, go0, go1 = [sums[:, n : n + 1] for n in range(6)]
    inverse = lax.rsqrt(rr * (1.0 / D) + eps)
    values = rg * inverse
    error = values - target
    pull = inverse * inverse * inverse * (error * rg * (1.0 / D))
    gw0 = route_scale * (inverse * error * go0 - pull * ro0)
    gw1 = route_scale * (inverse * error * go1 - pull * ro1)
    centre = w0 * gw0 + w1 * gw1
    gl0 = (gw0 - centre) / score_sum * first * (1.0 - first)
    gl1 = (gw1 - centre) / score_sum * second * (1.0 - second)
    both = jnp.concatenate([gl0, gl1], axis=0).astype(BF16).astype(F32)

    for j in range(NC):
        dlo[j] = jnp.sum(qs[j].astype(F32) * both, axis=0, keepdims=True)
        if j == plan.home:
            dli[own] = dlo[j]
        partners(j, lambda d, i, j=j: dl_copy(j, d, i).start())

    values_out[...] = jnp.transpose(jnp.broadcast_to(values, (T, LANES)))[0:1, :]
    values_store = pltpu.make_async_copy(values_out, values_ref, w_sem.at[10])
    values_store.start()
    sums_copy.wait_send()
    for j in range(NC):
        partners(j, lambda d, i, j=j: ret_copy(j, d, i).wait_send())

    grad = jnp.zeros((1, H), F32)
    for j in range(NC):
        partners(j, lambda d, i, j=j: dl_copy(j, d, i).wait_recv())
        got = dli[j * CD : (j + 1) * CD]
        mine = lax.broadcasted_iota(jnp.int32, (CD, 1, LANES), 0) == lane_i.reshape(1, 1, LANES)
        line = jnp.sum(jnp.where(mine, got, 0.0), axis=0)
        line = jnp.broadcast_to(line, (TILE, LANES)).astype(BF16)[:, 0:XR]
        grad = grad + jnp.dot(line, xs[j, c], preferred_element_type=F32)[0:1]

    row9[...] = jnp.zeros_like(row9)
    for q in range(plan.pieces):
        row9[q : q + 1, :] = grad[:, q * LANES : (q + 1) * LANES]
    zb[z] = row9[...].astype(BF16)

    def z_copy(dz):
        return pltpu.make_async_remote_copy(
            zb.at[z], zb.at[z], z_s.at[dz], z_r.at[z], (lax.rem(z + dz, NZ), me, c), MESH
        )

    def z_from(dz):
        source = lax.rem(z - dz + NZ, NZ)
        return pltpu.make_async_remote_copy(
            zb.at[source], zb.at[source], z_s.at[dz], z_r.at[source], (source, me, c), MESH
        )

    def z_start(dz, carry):
        z_copy(dz).start()
        return carry

    def z_wait(dz, carry):
        z_from(dz).wait_recv()
        return carry

    lax.fori_loop(1, NZ, z_start, 0)
    for j in range(NC):
        partners(j, lambda d, i, j=j: dl_copy(j, d, i).wait_send())
    values_store.wait()
    lax.fori_loop(1, NZ, z_wait, 0)
    grad = zb[0].astype(F32)
    for source in range(1, NZ):
        grad = grad + zb[source].astype(F32)

    agb[c, me] = grad.astype(BF16)

    def ag_copy(j, d, i):
        return pltpu.make_async_remote_copy(
            agb.at[c, me], agb.at[c, me], ag_s.at[d], ag_r.at[d], (z, ahead(j, i), c), MESH
        )

    def ag_from(j, d, i):
        source = behind(j, i)
        return pltpu.make_async_remote_copy(
            agb.at[c, source], agb.at[c, source], ag_s.at[d], ag_r.at[d], (z, source, c), MESH
        )

    for j in range(NC):
        partners(j, lambda d, i, j=j: ag_copy(j, d, i).start())

    def left_plane(dz, carry):
        z_copy(dz).wait_send()
        return carry

    lax.fori_loop(1, NZ, left_plane, 0)
    for j in range(NC):
        partners(j, lambda d, i, j=j: ag_from(j, d, i).wait_recv())
    agx = pltpu.make_async_remote_copy(
        agb.at[c], agb.at[c], agx_s, agx_r, (z, me, other), MESH
    )
    agx.start()

    def write(part, n):
        wide9[...] = agb[part].astype(F32).reshape(NE * TILE, LANES)
        for q in range(plan.pieces):
            lanes = slice(q * LANES, (q + 1) * LANES)
            grad_out[n, :, lanes] = wide9[pl.ds(q, NE, stride=TILE), :].astype(BF16)
        at = pl.ds(pl.multiple_of(part * H, LANES), H)
        store = pltpu.make_async_copy(grad_out.at[n], grad_ref.at[:, at], w_sem.at[11 + n])
        store.start()
        return store

    first = write(c, 0)
    for j in range(NC):
        partners(j, lambda d, i, j=j: ag_copy(j, d, i).wait_send())
    agx.wait()
    second = write(other, 1)
    first.wait()
    second.wait()


def on_device(
    mesh,
    tokens,
    routes,
    returns,
    router_weight,
    gate_weight,
    up_weight,
    down_weight,
    norm_gain,
    value_weight,
):
    count, width = tokens.shape
    hidden = gate_weight.shape[2]
    plan = Plan(mesh, count, width, hidden)
    NE, NC, H = plan.groups, plan.chunks, plan.half
    packed = (NE, TILE, plan.packed)
    vmem, dma = pltpu.VMEM, pltpu.SemaphoreType.DMA
    in_place = pl.BlockSpec(memory_space=pl.ANY)
    values, grad = pl.pallas_call(
        functools.partial(expert_kernel, plan),
        out_shape=(
            jax.ShapeDtypeStruct((1, count), F32),
            jax.ShapeDtypeStruct((NE, width), BF16),
        ),
        in_specs=[in_place] * 9,
        out_specs=(in_place, in_place),
        scratch_shapes=[
            vmem((count, width), BF16),
            vmem((2, count), jnp.int32),
            vmem((1, count), F32),
            vmem((NE, width), BF16),
            vmem((width,), F32),
            vmem((width,), BF16),
            vmem((1, width), F32),
            vmem((width, hidden), BF16),
            vmem((width, hidden), BF16),
            vmem((2, hidden, H), BF16),
            vmem(packed, BF16),
            vmem(packed, BF16),
            vmem(packed, BF16),
            vmem((NC, 2, plan.rows, H), BF16),
            vmem(packed, BF16),
            vmem(packed, BF16),
            vmem(packed, BF16),
            vmem(packed, BF16),
            vmem((NC, 2 * count, LANES), BF16),
            vmem((plan.rows, H), BF16),
            vmem((2 * count, H), F32),
            vmem((plan.each * TILE, LANES), F32),
            vmem((plan.each * TILE, LANES), F32),
            vmem((NE * TILE, LANES), F32),
            vmem((2, count, LANES), F32),
            vmem((count, LANES), F32),
            vmem((count, LANES), F32),
            vmem((NC, 1, LANES), F32),
            vmem((NE, 1, LANES), F32),
            vmem((plan.nz, TILE, LANES), BF16),
            vmem((TILE, LANES), F32),
            vmem((2, NE, TILE, LANES), BF16),
            vmem((1, count), F32),
            vmem((2, NE, H), BF16),
            dma((13,)),
            dma((NE,)),
            dma((NE,)),
            dma((NE,)),
            dma((NE,)),
            dma((NC,)),
            dma((NC,)),
            dma((NE,)),
            dma((NE,)),
            dma,
            dma,
            dma((NE,)),
            dma((NE,)),
            dma((plan.nz,)),
            dma((plan.nz,)),
            dma((NE,)),
            dma((NE,)),
            dma,
            dma,
        ],
        compiler_params=pltpu.CompilerParams(
            collective_id=0, has_side_effects=True, vmem_limit_bytes=60 * 1024 * 1024
        ),
        cost_estimate=pl.CostEstimate(
            flops=6 * NE * 9 * width * hidden,
            bytes_accessed=6 * width * hidden,
            transcendentals=NE * 9 * hidden,
        ),
    )(
        tokens,
        routes.T,
        returns.reshape(1, count),
        router_weight.T,
        gate_weight,
        up_weight,
        down_weight,
        norm_gain,
        value_weight,
    )
    return values.reshape(count), grad.T


def solution(mesh):
    return jax.shard_map(
        functools.partial(on_device, mesh),
        mesh=mesh,
        in_specs=(
            P(("dp", "expert"), None),
            P(("dp", "expert"), None),
            P(("dp", "expert")),
            P(),
            P("expert", None, "tensor"),
            P("expert", None, "tensor"),
            P("expert", "tensor", None),
            P(),
            P(),
        ),
        out_specs=(P(("dp", "expert")), P()),
        check_vma=False,
    )
```

```python
import functools
import jax
import jax.numpy as jnp
from jax import lax
from jax.experimental import pallas as pl
from jax.experimental.pallas import tpu as pltpu
from jax.sharding import PartitionSpec as P

MESH = pl.DeviceIdType.MESH
F32 = jnp.float32
BF16 = jnp.bfloat16
eps = 1e-06
route_scale = 2.5
LANES = 128
EIGHT = 8
TILE = 16


class Plan:
    def __init__(self, mesh, tokens, width, hidden):
        self.nz, self.groups = mesh.shape["dp"], mesh.shape["expert"]
        self.ny = 8 if self.groups >= 32 else 2
        self.nx = self.groups // self.ny
        self.steps = ((0, 4), (2, 6), (3, 5), (1, 7)) if self.ny == 8 else ((0,), (1,))
        self.chunks = len(self.steps)
        self.home = [one[0] for one in self.steps].index(0)
        self.each = self.groups // self.chunks
        self.tokens, self.width, self.hidden = tokens, width, hidden
        self.half = width // 2
        self.quarter = width // 4
        self.pieces = self.half // LANES
        self.packed = self.quarter + LANES
        self.main = self.each * EIGHT
        self.rows = self.main + max(TILE, self.each)


def expert_kernel(
    plan,
    tok_hbm,
    routes_hbm,
    returns_hbm,
    router_hbm,
    gate_hbm,
    up_hbm,
    down_hbm,
    gain_hbm,
    head_hbm,
    values_ref,
    grad_ref,
    tok_ref,
    routes_ref,
    returns_ref,
    router_ref,
    gain_ref,
    head_ref,
    gained_ref,
    wg,
    wu,
    wd,
    out,
    arr,
    oth,
    xs,
    pxo,
    pxi,
    ret,
    back,
    qs,
    answer,
    mix,
    nine,
    tmp9,
    wide9,
    chosen_ref,
    sums_out,
    sums_in,
    dlo,
    dli,
    zb,
    row9,
    agb,
    w_sem,
    out_s,
    out_r,
    fwd_s,
    fwd_r,
    px_s,
    px_r,
    ret_s,
    ret_r,
    sum_s,
    sum_r,
    dl_s,
    dl_r,
    z_s,
    z_r,
    ag_s,
    ag_r,
    agx_s,
    agx_r,
):
    T, D, H, Q4 = plan.tokens, plan.width, plan.half, plan.quarter
    NZ, NE, NX, NY = plan.nz, plan.groups, plan.nx, plan.ny
    NC, CD, MAIN, XR = plan.chunks, plan.each, plan.main, plan.rows
    z = lax.axis_index("dp")
    me = lax.axis_index("expert")
    c = lax.axis_index("tensor")
    other = 1 - c
    own = plan.home * plan.each
    mx, my = lax.div(me, NY), lax.rem(me, NY)

    def hops(j, i):
        dx, b = lax.rem(i, NX), lax.div(i, NX)
        first = plan.steps[j][0]
        return dx, (first + b * (plan.steps[j][1] - first) if len(plan.steps[j]) > 1 else first)

    def ahead(j, i):
        dx, dy = hops(j, i)
        return lax.rem(mx + dx, NX) * NY + lax.rem(my + dy, NY)

    def behind(j, i):
        dx, dy = hops(j, i)
        return lax.rem(mx - dx + NX, NX) * NY + lax.rem(my - dy + NY, NY)

    def partners(j, body):
        def run(i, carry):
            body(jnp.int32(j * CD) + i, i)
            return carry

        lax.fori_loop(1 if j == plan.home else 0, CD, run, 0)

    def load(source, target, n):
        return pltpu.make_async_copy(source, target, w_sem.at[n])

    route_load = load(routes_hbm, routes_ref, 0)
    route_load.start()
    token_load = load(tok_hbm, tok_ref, 1)
    token_load.start()

    barrier = pltpu.get_barrier_semaphore()
    for j in range(NC):
        partners(
            j,
            lambda d, i, j=j: pl.semaphore_signal(
                barrier, inc=1, device_id=(z, ahead(j, i), c), device_id_type=MESH
            ),
        )

    def greet(dz, carry):
        pl.semaphore_signal(
            barrier, inc=1, device_id=(lax.rem(z + dz, NZ), me, c), device_id_type=MESH
        )
        return carry

    lax.fori_loop(1, NZ, greet, 0)
    pl.semaphore_signal(barrier, inc=1, device_id=(z, me, other), device_id_type=MESH)

    small_loads = [
        load(router_hbm, router_ref, 2),
        load(returns_hbm, returns_ref, 3),
        load(gain_hbm, gain_ref, 4),
        load(head_hbm, head_ref, 5),
    ]
    weight_loads = [
        load(gate_hbm.at[0], wg, 6),
        load(up_hbm.at[0], wu, 7),
        load(down_hbm.at[0, :, pl.ds(0, H)], wd.at[0], 8),
        load(down_hbm.at[0, :, pl.ds(H, H)], wd.at[1], 9),
    ]
    for one in small_loads + weight_loads:
        one.start()

    def out_copy(j, d, i):
        return pltpu.make_async_remote_copy(
            out.at[d], arr.at[d], out_s.at[d], out_r.at[d], (z, ahead(j, i), c), MESH
        )

    def fwd_copy(d):
        return pltpu.make_async_remote_copy(
            arr.at[d], oth.at[d], fwd_s.at[d], fwd_r.at[d], (z, me, other), MESH
        )

    def px_copy(j):
        part = pl.ds(j * CD, CD)
        return pltpu.make_async_remote_copy(
            pxo.at[part], pxi.at[part], px_s.at[j], px_r.at[j], (z, me, other), MESH
        )

    def ret_copy(j, d, i):
        return pltpu.make_async_remote_copy(
            ret.at[d], back.at[d], ret_s.at[d], ret_r.at[d], (z, behind(j, i), c), MESH
        )

    def dl_copy(j, d, i):
        return pltpu.make_async_remote_copy(
            dlo.at[j], dli.at[d], dl_s.at[d], dl_r.at[d], (z, ahead(j, i), c), MESH
        )

    def partner_of(l):
        return jnp.where(l < MAIN, lax.shift_right_logical(l, 3), l - MAIN)

    def slot_of(l):
        slot = jnp.where(l < MAIN, jnp.bitwise_and(l, 7) + 1, EIGHT + 1)
        return jnp.where(l < MAIN + CD, slot, -1).astype(F32)

    def expert_of(l, j):
        i = partner_of(l)
        b = lax.shift_right_logical(i, NX.bit_length() - 1)
        dy = jnp.full(l.shape, plan.steps[j][0], jnp.int32)
        for n in range(1, len(plan.steps[j])):
            dy = jnp.where(b == n, plan.steps[j][n], dy)
        ex = jnp.bitwise_and(mx + jnp.bitwise_and(i, NX - 1), NX - 1)
        return ex * NY + jnp.bitwise_and(my + dy, NY - 1)

    lane = lax.broadcasted_iota(jnp.int32, (1, LANES), 1)
    lane_i, lane_slot = partner_of(lane), slot_of(lane)

    def pack(dst, j, rows):
        part = pl.ds(j * CD, CD)
        first = rows[0:MAIN, 0:Q4].reshape(CD, EIGHT, Q4)
        second = rows[0:MAIN, Q4:H].reshape(CD, EIGHT, Q4)
        dst[part, :, 0:Q4] = jnp.concatenate([first, second], axis=1).astype(BF16)
        for q in range(plan.pieces):
            nine[pl.ds(q, CD, stride=TILE), :] = rows[MAIN : MAIN + CD, q * LANES : (q + 1) * LANES]
        dst[part, :, Q4:] = nine[...].reshape(CD, TILE, LANES).astype(BF16)

    def unpack(src, j, put):
        part = pl.ds(j * CD, CD)
        both = src[part, :, 0:Q4].astype(F32)
        put(0, MAIN, 0, Q4, both[:, 0:EIGHT].reshape(MAIN, Q4).astype(BF16))
        put(0, MAIN, Q4, Q4, both[:, EIGHT:TILE].reshape(MAIN, Q4).astype(BF16))
        tmp9[...] = src[part, :, Q4:].astype(F32).reshape(CD * TILE, LANES)
        last = jnp.concatenate(
            [tmp9[pl.ds(q, CD, stride=TILE), :] for q in range(plan.pieces)], axis=1
        )
        last = jnp.concatenate([last, jnp.zeros((XR - MAIN - CD, H), F32)], axis=0)
        put(MAIN, XR - MAIN, 0, H, last.astype(BF16))

    nine[...] = jnp.zeros_like(nine)
    expert_row = lax.broadcasted_iota(jnp.int32, (NE, T), 0)
    before = (
        lax.broadcasted_iota(jnp.int32, (T, T), 0) < lax.broadcasted_iota(jnp.int32, (T, T), 1)
    ).astype(BF16)
    slot_row = lax.broadcasted_iota(jnp.int32, (XR, NE), 0)
    expert_column = lax.broadcasted_iota(jnp.int32, (XR, NE), 1)
    row_slot = slot_of(lax.broadcasted_iota(jnp.int32, (XR, T), 0))
    spreads = [(expert_column == expert_of(slot_row, j)).astype(BF16) for j in range(NC)]
    route_load.wait()
    named = (expert_row == routes_ref[0:1, :]) | (expert_row == routes_ref[1:2, :])
    named = named.astype(F32)
    earlier = jnp.dot(named.astype(BF16), before, preferred_element_type=F32)
    key = (named * (earlier + 1.0)).astype(BF16)
    picks = []
    for j in range(NC):
        spread = jnp.dot(spreads[j], key, preferred_element_type=F32)
        picks.append((spread == row_slot).astype(BF16))

    columns = pl.ds(pl.multiple_of(c * H, LANES), H)
    token_load.wait()
    for j in range(NC):
        pack(out, j, jnp.dot(picks[j], tok_ref[:, columns], preferred_element_type=F32))
        if j == 0:
            pl.semaphore_wait(barrier, NE - 1 + NZ - 1 + 1)
        partners(j, lambda d, i, j=j: out_copy(j, d, i).start())
        if j == plan.home:
            arr[own] = out[own]
            fwd_copy(own).start()

    marks = [
        jnp.transpose(
            (
                lax.broadcasted_iota(jnp.int32, (LANES, T), 0) == routes_ref[k : k + 1, :]
            ).astype(F32)
        )
        for k in range(2)
    ]
    after = (
        lax.broadcasted_iota(jnp.int32, (T, T), 0) > lax.broadcasted_iota(jnp.int32, (T, T), 1)
    ).astype(BF16)
    cum = jnp.dot(after, (marks[0] + marks[1]).astype(BF16), preferred_element_type=F32)
    key = jnp.concatenate([marks[0] * (cum + 1.0), marks[1] * (cum + 1.0)], axis=0).astype(BF16)
    for j in range(NC):
        spread = (lax.broadcasted_iota(jnp.int32, (LANES, LANES), 0) == expert_of(lane, j)).astype(
            BF16
        )
        spread = jnp.dot(key, spread, preferred_element_type=F32)
        qs[j] = (spread == lane_slot).astype(F32).astype(BF16)

    for one in small_loads:
        one.wait()
    for n in range(0, D, 2 * LANES):
        gained = gain_ref[n : n + 2 * LANES] * head_ref[n : n + 2 * LANES].astype(F32)
        gained_ref[:, n : n + 2 * LANES] = gained.reshape(1, 2 * LANES)
    logits = lax.dot_general(
        tok_ref[...], router_ref[...], (((1,), (1,)), ((), ())), preferred_element_type=F32
    )
    scores = jax.nn.sigmoid(logits)
    for k in range(2):
        chosen = jnp.sum(marks[k][:, 0:NE] * scores, axis=1, keepdims=True)
        chosen_ref[k] = jnp.broadcast_to(chosen, (T, LANES))

    for one in weight_loads:
        one.wait()

    for j in range(NC):

        def arrive(d, i, j=j):
            out_copy(j, d, i).wait_recv()
            fwd_copy(d).start()

        partners(j, arrive)

        def put_own(r, n, col, m, v, j=j):
            xs[j, c, r : r + n, col : col + m] = v

        def put_other(r, n, col, m, v, j=j):
            xs[j, other, r : r + n, col : col + m] = v

        unpack(arr, j, put_own)

        def forwarded(i, carry, j=j):
            fwd_copy(jnp.int32(j * CD) + i).wait_recv()
            return carry

        lax.fori_loop(0, CD, forwarded, 0)
        unpack(oth, j, put_other)
        gate = jnp.dot(xs[j, 0], wg[0:H, :], preferred_element_type=F32)
        gate = gate + jnp.dot(xs[j, 1], wg[H:D, :], preferred_element_type=F32)
        upward = jnp.dot(xs[j, 0], wu[0:H, :], preferred_element_type=F32)
        upward = upward + jnp.dot(xs[j, 1], wu[H:D, :], preferred_element_type=F32)
        hidden = (gate / (1.0 + jnp.exp(-gate)) * upward).astype(BF16)
        pack(pxo, j, jnp.dot(hidden, wd[other], preferred_element_type=F32))
        px_copy(j).start()
        pack(ret, j, jnp.dot(hidden, wd[c], preferred_element_type=F32))
        px_copy(j).wait_recv()
        part = pl.ds(j * CD, CD)
        ret[part] = (ret[part].astype(F32) + pxi[part].astype(F32)).astype(BF16)
        if j == plan.home:
            back[own] = ret[own]
        partners(j, lambda d, i, j=j: ret_copy(j, d, i).start())

    for j in range(NC):
        px_copy(j).wait_send()
        partners(j, lambda d, i, j=j: out_copy(j, d, i).wait_send())

    def left_chip(d, carry):
        fwd_copy(d).wait_send()
        return carry

    lax.fori_loop(0, NE, left_chip, 0)

    def put_answer(r, n, col, m, v):
        answer[r : r + n, col : col + m] = v

    for j in range(NC):
        partners(j, lambda d, i, j=j: ret_copy(j, d, i).wait_recv())
        unpack(back, j, put_answer)
        term = jnp.dot(qs[j][:, 0:XR], answer[...], preferred_element_type=F32)
        if j == 0:
            mix[...] = term
        else:
            mix[...] += term

    block = min(32, T)
    for b in range(T // block):
        low, high = b * block, (b + 1) * block
        first, second = chosen_ref[0, low:high], chosen_ref[1, low:high]
        total = first + second
        w0, w1 = first / total, second / total
        acc = [jnp.zeros((block, LANES), F32) for _ in range(6)]
        for q in range(plan.pieces):
            at = pl.ds(pl.multiple_of(c * H + q * LANES, LANES), LANES)
            gained = gained_ref[:, at]
            o0 = mix[low:high, q * LANES : (q + 1) * LANES]
            o1 = mix[T + low : T + high, q * LANES : (q + 1) * LANES]
            residual = tok_ref[low:high, at].astype(F32) + route_scale * (w0 * o0 + w1 * o1)
            terms = (
                residual * residual,
                residual * gained,
                residual * o0,
                residual * o1,
                gained * o0,
                gained * o1,
            )
            acc = [a + term for a, term in zip(acc, terms)]
        line = jnp.zeros((block, LANES), F32)
        for n, a in enumerate(acc):
            line = jnp.where(lane == n, jnp.sum(a, axis=1, keepdims=True), line)
        sums_out[low:high, :] = line

    sums_copy = pltpu.make_async_remote_copy(
        sums_out, sums_in, sum_s, sum_r, (z, me, other), MESH
    )
    sums_copy.start()
    raw = jnp.transpose(jnp.broadcast_to(returns_ref[...], (LANES, T)))[:, 0:1]
    sign = jnp.where(raw > 0.0, 1.0, jnp.where(raw < 0.0, -1.0, 0.0))
    target = sign * (jnp.sqrt(jnp.abs(raw) + 1.0) - 1.0) + 0.001 * raw
    first, second = chosen_ref[0][:, 0:1], chosen_ref[1][:, 0:1]
    score_sum = first + second
    w0, w1 = first / score_sum, second / score_sum
    sums_copy.wait_recv()
    sums = sums_out[...] + sums_in[...]
    rr, rg, ro0, ro1, go0, go1 = [sums[:, n : n + 1] for n in range(6)]
    inverse = lax.rsqrt(rr * (1.0 / D) + eps)
    values = rg * inverse
    error = values - target
    pull = inverse * inverse * inverse * (error * rg * (1.0 / D))
    gw0 = route_scale * (inverse * error * go0 - pull * ro0)
    gw1 = route_scale * (inverse * error * go1 - pull * ro1)
    centre = w0 * gw0 + w1 * gw1
    gl0 = (gw0 - centre) / score_sum * first * (1.0 - first)
    gl1 = (gw1 - centre) / score_sum * second * (1.0 - second)
    both = jnp.concatenate([gl0, gl1], axis=0).astype(BF16).astype(F32)

    for j in range(NC):
        dlo[j] = jnp.sum(qs[j].astype(F32) * both, axis=0, keepdims=True)
        if j == plan.home:
            dli[own] = dlo[j]
        partners(j, lambda d, i, j=j: dl_copy(j, d, i).start())

    values_ref[...] = jnp.transpose(jnp.broadcast_to(values, (T, LANES)))[0:1, :]
    sums_copy.wait_send()
    for j in range(NC):
        partners(j, lambda d, i, j=j: ret_copy(j, d, i).wait_send())

    grad = jnp.zeros((1, H), F32)
    for j in range(NC):
        partners(j, lambda d, i, j=j: dl_copy(j, d, i).wait_recv())
        got = dli[j * CD : (j + 1) * CD]
        mine = lax.broadcasted_iota(jnp.int32, (CD, 1, LANES), 0) == lane_i.reshape(1, 1, LANES)
        line = jnp.sum(jnp.where(mine, got, 0.0), axis=0)
        line = jnp.broadcast_to(line, (TILE, LANES)).astype(BF16)[:, 0:XR]
        grad = grad + jnp.dot(line, xs[j, c], preferred_element_type=F32)[0:1]

    row9[...] = jnp.zeros_like(row9)
    for q in range(plan.pieces):
        row9[q : q + 1, :] = grad[:, q * LANES : (q + 1) * LANES]
    zb[z] = row9[...].astype(BF16)

    def z_copy(dz):
        return pltpu.make_async_remote_copy(
            zb.at[z], zb.at[z], z_s.at[dz], z_r.at[z], (lax.rem(z + dz, NZ), me, c), MESH
        )

    def z_from(dz):
        source = lax.rem(z - dz + NZ, NZ)
        return pltpu.make_async_remote_copy(
            zb.at[source], zb.at[source], z_s.at[dz], z_r.at[source], (source, me, c), MESH
        )

    def z_start(dz, carry):
        z_copy(dz).start()
        return carry

    def z_wait(dz, carry):
        z_from(dz).wait_recv()
        return carry

    lax.fori_loop(1, NZ, z_start, 0)
    for j in range(NC):
        partners(j, lambda d, i, j=j: dl_copy(j, d, i).wait_send())
    lax.fori_loop(1, NZ, z_wait, 0)
    grad = zb[0].astype(F32)
    for source in range(1, NZ):
        grad = grad + zb[source].astype(F32)

    agb[c, me] = grad.astype(BF16)

    def ag_copy(j, d, i):
        return pltpu.make_async_remote_copy(
            agb.at[c, me], agb.at[c, me], ag_s.at[d], ag_r.at[d], (z, ahead(j, i), c), MESH
        )

    def ag_from(j, d, i):
        source = behind(j, i)
        return pltpu.make_async_remote_copy(
            agb.at[c, source], agb.at[c, source], ag_s.at[d], ag_r.at[d], (z, source, c), MESH
        )

    for j in range(NC):
        partners(j, lambda d, i, j=j: ag_copy(j, d, i).start())

    def left_plane(dz, carry):
        z_copy(dz).wait_send()
        return carry

    lax.fori_loop(1, NZ, left_plane, 0)
    for j in range(NC):
        partners(j, lambda d, i, j=j: ag_from(j, d, i).wait_recv())
    agx = pltpu.make_async_remote_copy(
        agb.at[c], agb.at[c], agx_s, agx_r, (z, me, other), MESH
    )
    agx.start()

    def write(part):
        wide9[...] = agb[part].astype(F32).reshape(NE * TILE, LANES)
        for q in range(plan.pieces):
            at = pl.ds(pl.multiple_of(part * H + q * LANES, LANES), LANES)
            grad_ref[:, at] = wide9[pl.ds(q, NE, stride=TILE), :].astype(BF16)

    write(c)
    for j in range(NC):
        partners(j, lambda d, i, j=j: ag_copy(j, d, i).wait_send())
    agx.wait()
    write(other)


def on_device(
    mesh,
    tokens,
    routes,
    returns,
    router_weight,
    gate_weight,
    up_weight,
    down_weight,
    norm_gain,
    value_weight,
):
    count, width = tokens.shape
    hidden = gate_weight.shape[2]
    plan = Plan(mesh, count, width, hidden)
    NE, NC, H = plan.groups, plan.chunks, plan.half
    packed = (NE, TILE, plan.packed)
    vmem, dma = pltpu.VMEM, pltpu.SemaphoreType.DMA
    in_place = pl.BlockSpec(memory_space=pl.ANY)
    values, grad = pl.pallas_call(
        functools.partial(expert_kernel, plan),
        out_shape=(
            jax.ShapeDtypeStruct((1, count), F32),
            jax.ShapeDtypeStruct((NE, width), BF16),
        ),
        in_specs=[in_place] * 9,
        out_specs=(pl.BlockSpec(memory_space=pltpu.VMEM),) * 2,
        scratch_shapes=[
            vmem((count, width), BF16),
            vmem((2, count), jnp.int32),
            vmem((1, count), F32),
            vmem((NE, width), BF16),
            vmem((width,), F32),
            vmem((width,), BF16),
            vmem((1, width), F32),
            vmem((width, hidden), BF16),
            vmem((width, hidden), BF16),
            vmem((2, hidden, H), BF16),
            vmem(packed, BF16),
            vmem(packed, BF16),
            vmem(packed, BF16),
            vmem((NC, 2, plan.rows, H), BF16),
            vmem(packed, BF16),
            vmem(packed, BF16),
            vmem(packed, BF16),
            vmem(packed, BF16),
            vmem((NC, 2 * count, LANES), BF16),
            vmem((plan.rows, H), BF16),
            vmem((2 * count, H), F32),
            vmem((plan.each * TILE, LANES), F32),
            vmem((plan.each * TILE, LANES), F32),
            vmem((NE * TILE, LANES), F32),
            vmem((2, count, LANES), F32),
            vmem((count, LANES), F32),
            vmem((count, LANES), F32),
            vmem((NC, 1, LANES), F32),
            vmem((NE, 1, LANES), F32),
            vmem((plan.nz, TILE, LANES), BF16),
            vmem((TILE, LANES), F32),
            vmem((2, NE, TILE, LANES), BF16),
            dma((10,)),
            dma((NE,)),
            dma((NE,)),
            dma((NE,)),
            dma((NE,)),
            dma((NC,)),
            dma((NC,)),
            dma((NE,)),
            dma((NE,)),
            dma,
            dma,
            dma((NE,)),
            dma((NE,)),
            dma((plan.nz,)),
            dma((plan.nz,)),
            dma((NE,)),
            dma((NE,)),
            dma,
            dma,
        ],
        compiler_params=pltpu.CompilerParams(
            collective_id=0, has_side_effects=True, vmem_limit_bytes=48 * 1024 * 1024
        ),
        cost_estimate=pl.CostEstimate(
            flops=6 * NE * 9 * width * hidden,
            bytes_accessed=6 * width * hidden,
            transcendentals=NE * 9 * hidden,
        ),
    )(
        *(
            pltpu.with_memory_space_constraint(operand, pltpu.HBM)
            for operand in (
                tokens,
                routes.T,
                returns.reshape(1, count),
                router_weight.T,
                gate_weight,
                up_weight,
                down_weight,
                norm_gain,
                value_weight,
            )
        )
    )
    return values.reshape(count), grad.T


def solution(mesh):
    return jax.shard_map(
        functools.partial(on_device, mesh),
        mesh=mesh,
        in_specs=(
            P(("dp", "expert"), None),
            P(("dp", "expert"), None),
            P(("dp", "expert")),
            P(),
            P("expert", None, "tensor"),
            P("expert", None, "tensor"),
            P("expert", "tensor", None),
            P(),
            P(),
        ),
        out_specs=(P(("dp", "expert")), P()),
        check_vma=False,
    )
```

```python
import functools
import jax
import jax.numpy as jnp
from jax import lax
from jax.experimental import pallas as pl
from jax.experimental.pallas import tpu as pltpu
from jax.sharding import PartitionSpec as P

MESH = pl.DeviceIdType.MESH
F32 = jnp.float32
BF16 = jnp.bfloat16
eps = 1e-06
route_scale = 2.5
LANES = 128
EIGHT = 8
TILE = 16


class Plan:
    def __init__(self, mesh, tokens, width, hidden):
        self.nz, self.groups = mesh.shape["dp"], mesh.shape["expert"]
        self.ny = 8 if self.groups >= 32 else 2
        self.nx = self.groups // self.ny
        self.steps = ((0, 4), (2, 6), (3, 5), (1, 7)) if self.ny == 8 else ((0,), (1,))
        self.chunks = len(self.steps)
        self.joined = ((0, 1, 2), (3,)) if self.chunks == 4 else ((0, 1),)
        self.home = [one[0] for one in self.steps].index(0)
        self.each = self.groups // self.chunks
        self.tokens, self.width, self.hidden = tokens, width, hidden
        self.half = width // 2
        self.quarter = width // 4
        self.pieces = self.half // LANES
        self.packed = self.quarter + LANES
        self.main = self.each * EIGHT
        self.rows = self.main + max(TILE, self.each)


def expert_kernel(
    plan,
    tok_hbm,
    routes_hbm,
    returns_hbm,
    router_hbm,
    gate_hbm,
    up_hbm,
    down_hbm,
    gain_hbm,
    head_hbm,
    values_ref,
    grad_ref,
    tok_ref,
    routes_ref,
    returns_ref,
    router_ref,
    gain_ref,
    head_ref,
    gained_ref,
    wg,
    wu,
    wd,
    out,
    arr,
    oth,
    xs,
    pxo,
    pxi,
    ret,
    back,
    qs,
    joined,
    answer,
    mix,
    nine,
    tmp9,
    wide9,
    chosen_ref,
    sums_out,
    sums_in,
    dlo,
    dli,
    zb,
    row9,
    agb,
    w_sem,
    out_s,
    out_r,
    fwd_s,
    fwd_r,
    px_s,
    px_r,
    ret_s,
    ret_r,
    sum_s,
    sum_r,
    dl_s,
    dl_r,
    z_s,
    z_r,
    ag_s,
    ag_r,
    agx_s,
    agx_r,
):
    T, D, H, Q4 = plan.tokens, plan.width, plan.half, plan.quarter
    NZ, NE, NX, NY = plan.nz, plan.groups, plan.nx, plan.ny
    NC, CD, MAIN, XR = plan.chunks, plan.each, plan.main, plan.rows
    z = lax.axis_index("dp")
    me = lax.axis_index("expert")
    c = lax.axis_index("tensor")
    other = 1 - c
    own = plan.home * plan.each
    mx, my = lax.div(me, NY), lax.rem(me, NY)

    def hops(j, i):
        dx, b = lax.rem(i, NX), lax.div(i, NX)
        first = plan.steps[j][0]
        return dx, (first + b * (plan.steps[j][1] - first) if len(plan.steps[j]) > 1 else first)

    def ahead(j, i):
        dx, dy = hops(j, i)
        return lax.rem(mx + dx, NX) * NY + lax.rem(my + dy, NY)

    def behind(j, i):
        dx, dy = hops(j, i)
        return lax.rem(mx - dx + NX, NX) * NY + lax.rem(my - dy + NY, NY)

    def partners(j, body):
        def run(i, carry):
            body(jnp.int32(j * CD) + i, i)
            return carry

        lax.fori_loop(1 if j == plan.home else 0, CD, run, 0)

    def load(source, target, n):
        return pltpu.make_async_copy(source, target, w_sem.at[n])

    route_load = load(routes_hbm, routes_ref, 0)
    route_load.start()
    token_load = load(tok_hbm, tok_ref, 1)
    token_load.start()

    barrier = pltpu.get_barrier_semaphore()
    for j in range(NC):
        partners(
            j,
            lambda d, i, j=j: pl.semaphore_signal(
                barrier, inc=1, device_id=(z, ahead(j, i), c), device_id_type=MESH
            ),
        )

    def greet(dz, carry):
        pl.semaphore_signal(
            barrier, inc=1, device_id=(lax.rem(z + dz, NZ), me, c), device_id_type=MESH
        )
        return carry

    lax.fori_loop(1, NZ, greet, 0)
    pl.semaphore_signal(barrier, inc=1, device_id=(z, me, other), device_id_type=MESH)

    small_loads = [
        load(router_hbm, router_ref, 2),
        load(returns_hbm, returns_ref, 3),
        load(gain_hbm, gain_ref, 4),
        load(head_hbm, head_ref, 5),
    ]
    weight_loads = [
        load(gate_hbm.at[0], wg, 6),
        load(up_hbm.at[0], wu, 7),
        load(down_hbm.at[0, :, pl.ds(0, H)], wd.at[0], 8),
        load(down_hbm.at[0, :, pl.ds(H, H)], wd.at[1], 9),
    ]
    for one in small_loads + weight_loads:
        one.start()

    def out_copy(j, d, i):
        return pltpu.make_async_remote_copy(
            out.at[d], arr.at[d], out_s.at[d], out_r.at[d], (z, ahead(j, i), c), MESH
        )

    def fwd_copy(d):
        return pltpu.make_async_remote_copy(
            arr.at[d], oth.at[d], fwd_s.at[d], fwd_r.at[d], (z, me, other), MESH
        )

    def px_copy(j):
        part = pl.ds(j * CD, CD)
        return pltpu.make_async_remote_copy(
            pxo.at[part], pxi.at[part], px_s.at[j], px_r.at[j], (z, me, other), MESH
        )

    def ret_copy(j, d, i):
        return pltpu.make_async_remote_copy(
            ret.at[d], back.at[d], ret_s.at[d], ret_r.at[d], (z, behind(j, i), c), MESH
        )

    def dl_copy(j, d, i):
        return pltpu.make_async_remote_copy(
            dlo.at[j], dli.at[d], dl_s.at[d], dl_r.at[d], (z, ahead(j, i), c), MESH
        )

    def partner_of(l):
        return jnp.where(l < MAIN, lax.shift_right_logical(l, 3), l - MAIN)

    def slot_of(l):
        slot = jnp.where(l < MAIN, jnp.bitwise_and(l, 7) + 1, EIGHT + 1)
        return jnp.where(l < MAIN + CD, slot, -1).astype(F32)

    def expert_of(l, j):
        i = partner_of(l)
        b = lax.shift_right_logical(i, NX.bit_length() - 1)
        dy = jnp.full(l.shape, plan.steps[j][0], jnp.int32)
        for n in range(1, len(plan.steps[j])):
            dy = jnp.where(b == n, plan.steps[j][n], dy)
        ex = jnp.bitwise_and(mx + jnp.bitwise_and(i, NX - 1), NX - 1)
        return ex * NY + jnp.bitwise_and(my + dy, NY - 1)

    lane = lax.broadcasted_iota(jnp.int32, (1, LANES), 1)
    lane_i, lane_slot = partner_of(lane), slot_of(lane)

    def pack(dst, j, rows):
        part = pl.ds(j * CD, CD)
        first = rows[0:MAIN, 0:Q4].reshape(CD, EIGHT, Q4)
        second = rows[0:MAIN, Q4:H].reshape(CD, EIGHT, Q4)
        dst[part, :, 0:Q4] = jnp.concatenate([first, second], axis=1).astype(BF16)
        for q in range(plan.pieces):
            nine[pl.ds(q, CD, stride=TILE), :] = rows[MAIN : MAIN + CD, q * LANES : (q + 1) * LANES]
        dst[part, :, Q4:] = nine[...].reshape(CD, TILE, LANES).astype(BF16)

    def unpack(src, j, put):
        part = pl.ds(j * CD, CD)
        both = src[part, :, 0:Q4].astype(F32)
        put(0, MAIN, 0, Q4, both[:, 0:EIGHT].reshape(MAIN, Q4).astype(BF16))
        put(0, MAIN, Q4, Q4, both[:, EIGHT:TILE].reshape(MAIN, Q4).astype(BF16))
        tmp9[...] = src[part, :, Q4:].astype(F32).reshape(CD * TILE, LANES)
        last = jnp.concatenate(
            [tmp9[pl.ds(q, CD, stride=TILE), :] for q in range(plan.pieces)], axis=1
        )
        last = jnp.concatenate([last, jnp.zeros((XR - MAIN - CD, H), F32)], axis=0)
        put(MAIN, XR - MAIN, 0, H, last.astype(BF16))

    nine[...] = jnp.zeros_like(nine)
    expert_row = lax.broadcasted_iota(jnp.int32, (NE, T), 0)
    before = (
        lax.broadcasted_iota(jnp.int32, (T, T), 0) < lax.broadcasted_iota(jnp.int32, (T, T), 1)
    ).astype(BF16)
    slot_row = lax.broadcasted_iota(jnp.int32, (XR, NE), 0)
    expert_column = lax.broadcasted_iota(jnp.int32, (XR, NE), 1)
    row_slot = slot_of(lax.broadcasted_iota(jnp.int32, (XR, T), 0))
    spreads = [(expert_column == expert_of(slot_row, j)).astype(BF16) for j in range(NC)]
    route_load.wait()
    named = (expert_row == routes_ref[0:1, :]) | (expert_row == routes_ref[1:2, :])
    named = named.astype(F32)
    earlier = jnp.dot(named.astype(BF16), before, preferred_element_type=F32)
    key = (named * (earlier + 1.0)).astype(BF16)
    picks = []
    for j in range(NC):
        spread = jnp.dot(spreads[j], key, preferred_element_type=F32)
        picks.append((spread == row_slot).astype(BF16))

    columns = pl.ds(pl.multiple_of(c * H, LANES), H)
    token_load.wait()
    for j in range(NC):
        pack(out, j, jnp.dot(picks[j], tok_ref[:, columns], preferred_element_type=F32))
        if j == 0:
            pl.semaphore_wait(barrier, NE - 1 + NZ - 1 + 1)
        partners(j, lambda d, i, j=j: out_copy(j, d, i).start())
        if j == plan.home:
            arr[own] = out[own]
            fwd_copy(own).start()

    marks = [
        jnp.transpose(
            (
                lax.broadcasted_iota(jnp.int32, (LANES, T), 0) == routes_ref[k : k + 1, :]
            ).astype(F32)
        )
        for k in range(2)
    ]
    after = (
        lax.broadcasted_iota(jnp.int32, (T, T), 0) > lax.broadcasted_iota(jnp.int32, (T, T), 1)
    ).astype(BF16)
    cum = jnp.dot(after, (marks[0] + marks[1]).astype(BF16), preferred_element_type=F32)
    key = jnp.concatenate([marks[0] * (cum + 1.0), marks[1] * (cum + 1.0)], axis=0).astype(BF16)
    places = []
    for j in range(NC):
        spread = (lax.broadcasted_iota(jnp.int32, (LANES, LANES), 0) == expert_of(lane, j)).astype(
            BF16
        )
        spread = jnp.dot(key, spread, preferred_element_type=F32)
        place = (spread == lane_slot).astype(F32)
        qs[j] = place.astype(BF16)
        places.append(place[:, 0:XR])
    for n, steps in enumerate(plan.joined):
        place = jnp.concatenate([places[j] for j in steps], axis=1)
        joined[n, :, 0 : len(steps) * XR] = place.astype(BF16)

    for one in small_loads:
        one.wait()
    for n in range(0, D, 2 * LANES):
        gained = gain_ref[n : n + 2 * LANES] * head_ref[n : n + 2 * LANES].astype(F32)
        gained_ref[:, n : n + 2 * LANES] = gained.reshape(1, 2 * LANES)
    logits = lax.dot_general(
        tok_ref[...], router_ref[...], (((1,), (1,)), ((), ())), preferred_element_type=F32
    )
    scores = jax.nn.sigmoid(logits)
    for k in range(2):
        chosen = jnp.sum(marks[k][:, 0:NE] * scores, axis=1, keepdims=True)
        chosen_ref[k] = jnp.broadcast_to(chosen, (T, LANES))

    for one in weight_loads:
        one.wait()

    for j in range(NC):

        def arrive(d, i, j=j):
            out_copy(j, d, i).wait_recv()
            fwd_copy(d).start()

        partners(j, arrive)

        def put_own(r, n, col, m, v, j=j):
            xs[j, c, r : r + n, col : col + m] = v

        def put_other(r, n, col, m, v, j=j):
            xs[j, other, r : r + n, col : col + m] = v

        unpack(arr, j, put_own)

        def forwarded(i, carry, j=j):
            fwd_copy(jnp.int32(j * CD) + i).wait_recv()
            return carry

        lax.fori_loop(0, CD, forwarded, 0)
        unpack(oth, j, put_other)
        gate = jnp.dot(xs[j, 0], wg[0:H, :], preferred_element_type=F32)
        gate = gate + jnp.dot(xs[j, 1], wg[H:D, :], preferred_element_type=F32)
        upward = jnp.dot(xs[j, 0], wu[0:H, :], preferred_element_type=F32)
        upward = upward + jnp.dot(xs[j, 1], wu[H:D, :], preferred_element_type=F32)
        hidden = (gate / (1.0 + jnp.exp(-gate)) * upward).astype(BF16)
        pack(pxo, j, jnp.dot(hidden, wd[other], preferred_element_type=F32))
        px_copy(j).start()
        pack(ret, j, jnp.dot(hidden, wd[c], preferred_element_type=F32))
        px_copy(j).wait_recv()
        part = pl.ds(j * CD, CD)
        ret[part] = (ret[part].astype(F32) + pxi[part].astype(F32)).astype(BF16)
        if j == plan.home:
            back[own] = ret[own]
        partners(j, lambda d, i, j=j: ret_copy(j, d, i).start())

    for j in range(NC):
        px_copy(j).wait_send()
        partners(j, lambda d, i, j=j: out_copy(j, d, i).wait_send())

    def left_chip(d, carry):
        fwd_copy(d).wait_send()
        return carry

    lax.fori_loop(0, NE, left_chip, 0)

    for n, steps in enumerate(plan.joined):
        for k, j in enumerate(steps):

            def put_answer(r, rows, col, m, v, first=k * XR):
                answer[first + r : first + r + rows, col : col + m] = v

            partners(j, lambda d, i, j=j: ret_copy(j, d, i).wait_recv())
            unpack(back, j, put_answer)
        deep = len(steps) * XR
        term = jnp.dot(joined[n, :, 0:deep], answer[0:deep], preferred_element_type=F32)
        if n == 0:
            mix[...] = term
        else:
            mix[...] += term

    block = min(32, T)
    for b in range(T // block):
        low, high = b * block, (b + 1) * block
        first, second = chosen_ref[0, low:high], chosen_ref[1, low:high]
        total = first + second
        w0, w1 = first / total, second / total
        acc = [jnp.zeros((block, LANES), F32) for _ in range(6)]
        for q in range(plan.pieces):
            at = pl.ds(pl.multiple_of(c * H + q * LANES, LANES), LANES)
            gained = gained_ref[:, at]
            o0 = mix[low:high, q * LANES : (q + 1) * LANES]
            o1 = mix[T + low : T + high, q * LANES : (q + 1) * LANES]
            residual = tok_ref[low:high, at].astype(F32) + route_scale * (w0 * o0 + w1 * o1)
            terms = (
                residual * residual,
                residual * gained,
                residual * o0,
                residual * o1,
                gained * o0,
                gained * o1,
            )
            acc = [a + term for a, term in zip(acc, terms)]
        line = jnp.zeros((block, LANES), F32)
        for n, a in enumerate(acc):
            line = jnp.where(lane == n, jnp.sum(a, axis=1, keepdims=True), line)
        sums_out[low:high, :] = line

    sums_copy = pltpu.make_async_remote_copy(
        sums_out, sums_in, sum_s, sum_r, (z, me, other), MESH
    )
    sums_copy.start()
    raw = jnp.transpose(jnp.broadcast_to(returns_ref[...], (LANES, T)))[:, 0:1]
    sign = jnp.where(raw > 0.0, 1.0, jnp.where(raw < 0.0, -1.0, 0.0))
    target = sign * (jnp.sqrt(jnp.abs(raw) + 1.0) - 1.0) + 0.001 * raw
    first, second = chosen_ref[0][:, 0:1], chosen_ref[1][:, 0:1]
    score_sum = first + second
    w0, w1 = first / score_sum, second / score_sum
    sums_copy.wait_recv()
    sums = sums_out[...] + sums_in[...]
    rr, rg, ro0, ro1, go0, go1 = [sums[:, n : n + 1] for n in range(6)]
    inverse = lax.rsqrt(rr * (1.0 / D) + eps)
    values = rg * inverse
    error = values - target
    pull = inverse * inverse * inverse * (error * rg * (1.0 / D))
    gw0 = route_scale * (inverse * error * go0 - pull * ro0)
    gw1 = route_scale * (inverse * error * go1 - pull * ro1)
    centre = w0 * gw0 + w1 * gw1
    gl0 = (gw0 - centre) / score_sum * first * (1.0 - first)
    gl1 = (gw1 - centre) / score_sum * second * (1.0 - second)
    both = jnp.concatenate([gl0, gl1], axis=0).astype(BF16).astype(F32)

    for j in range(NC):
        dlo[j] = jnp.sum(qs[j].astype(F32) * both, axis=0, keepdims=True)
        if j == plan.home:
            dli[own] = dlo[j]
        partners(j, lambda d, i, j=j: dl_copy(j, d, i).start())

    values_ref[...] = jnp.transpose(jnp.broadcast_to(values, (T, LANES)))[0:1, :]
    sums_copy.wait_send()
    for j in range(NC):
        partners(j, lambda d, i, j=j: ret_copy(j, d, i).wait_send())

    grad = jnp.zeros((1, H), F32)
    for j in range(NC):
        partners(j, lambda d, i, j=j: dl_copy(j, d, i).wait_recv())
        got = dli[j * CD : (j + 1) * CD]
        mine = lax.broadcasted_iota(jnp.int32, (CD, 1, LANES), 0) == lane_i.reshape(1, 1, LANES)
        line = jnp.sum(jnp.where(mine, got, 0.0), axis=0)
        line = jnp.broadcast_to(line, (TILE, LANES)).astype(BF16)[:, 0:XR]
        grad = grad + jnp.dot(line, xs[j, c], preferred_element_type=F32)[0:1]

    row9[...] = jnp.zeros_like(row9)
    for q in range(plan.pieces):
        row9[q : q + 1, :] = grad[:, q * LANES : (q + 1) * LANES]
    zb[z] = row9[...].astype(BF16)

    def z_copy(n):
        dz = lax.rem(n + NZ // 2 - 1, NZ - 1) + 1
        return pltpu.make_async_remote_copy(
            zb.at[z], zb.at[z], z_s.at[n], z_r.at[z], (lax.rem(z + dz, NZ), me, c), MESH
        )

    def z_from(dz):
        source = lax.rem(z - dz + NZ, NZ)
        return pltpu.make_async_remote_copy(
            zb.at[source], zb.at[source], z_s.at[dz], z_r.at[source], (source, me, c), MESH
        )

    def z_start(dz, carry):
        z_copy(dz).start()
        return carry

    def z_wait(dz, carry):
        z_from(dz).wait_recv()
        return carry

    lax.fori_loop(1, NZ, z_start, 0)
    for j in range(NC):
        partners(j, lambda d, i, j=j: dl_copy(j, d, i).wait_send())
    lax.fori_loop(1, NZ, z_wait, 0)
    grad = zb[0].astype(F32)
    for source in range(1, NZ):
        grad = grad + zb[source].astype(F32)

    agb[c, me] = grad.astype(BF16)

    def ag_copy(j, d, i):
        return pltpu.make_async_remote_copy(
            agb.at[c, me], agb.at[c, me], ag_s.at[d], ag_r.at[d], (z, ahead(j, i), c), MESH
        )

    def ag_from(j, d, i):
        source = behind(j, i)
        return pltpu.make_async_remote_copy(
            agb.at[c, source], agb.at[c, source], ag_s.at[d], ag_r.at[d], (z, source, c), MESH
        )

    for j in range(NC):
        partners(j, lambda d, i, j=j: ag_copy(j, d, i).start())

    def left_plane(dz, carry):
        z_copy(dz).wait_send()
        return carry

    lax.fori_loop(1, NZ, left_plane, 0)
    for j in range(NC):
        partners(j, lambda d, i, j=j: ag_from(j, d, i).wait_recv())
    agx = pltpu.make_async_remote_copy(
        agb.at[c], agb.at[c], agx_s, agx_r, (z, me, other), MESH
    )
    agx.start()

    def write(part):
        wide9[...] = agb[part].astype(F32).reshape(NE * TILE, LANES)
        for q in range(plan.pieces):
            at = pl.ds(pl.multiple_of(part * H + q * LANES, LANES), LANES)
            grad_ref[:, at] = wide9[pl.ds(q, NE, stride=TILE), :].astype(BF16)

    write(c)
    for j in range(NC):
        partners(j, lambda d, i, j=j: ag_copy(j, d, i).wait_send())
    agx.wait()
    write(other)


def on_device(
    mesh,
    tokens,
    routes,
    returns,
    router_weight,
    gate_weight,
    up_weight,
    down_weight,
    norm_gain,
    value_weight,
):
    count, width = tokens.shape
    hidden = gate_weight.shape[2]
    plan = Plan(mesh, count, width, hidden)
    NE, NC, H = plan.groups, plan.chunks, plan.half
    packed = (NE, TILE, plan.packed)
    vmem, dma = pltpu.VMEM, pltpu.SemaphoreType.DMA
    in_place = pl.BlockSpec(memory_space=pl.ANY)
    values, grad = pl.pallas_call(
        functools.partial(expert_kernel, plan),
        out_shape=(
            jax.ShapeDtypeStruct((1, count), F32),
            jax.ShapeDtypeStruct((NE, width), BF16),
        ),
        in_specs=[in_place] * 9,
        out_specs=(pl.BlockSpec(memory_space=pltpu.VMEM),) * 2,
        scratch_shapes=[
            vmem((count, width), BF16),
            vmem((2, count), jnp.int32),
            vmem((1, count), F32),
            vmem((NE, width), BF16),
            vmem((width,), F32),
            vmem((width,), BF16),
            vmem((1, width), F32),
            vmem((width, hidden), BF16),
            vmem((width, hidden), BF16),
            vmem((2, hidden, H), BF16),
            vmem(packed, BF16),
            vmem(packed, BF16),
            vmem(packed, BF16),
            vmem((NC, 2, plan.rows, H), BF16),
            vmem(packed, BF16),
            vmem(packed, BF16),
            vmem(packed, BF16),
            vmem(packed, BF16),
            vmem((NC, 2 * count, LANES), BF16),
            vmem((len(plan.joined), 2 * count, 2 * LANES), BF16),
            vmem((max(map(len, plan.joined)) * plan.rows, H), BF16),
            vmem((2 * count, H), F32),
            vmem((plan.each * TILE, LANES), F32),
            vmem((plan.each * TILE, LANES), F32),
            vmem((NE * TILE, LANES), F32),
            vmem((2, count, LANES), F32),
            vmem((count, LANES), F32),
            vmem((count, LANES), F32),
            vmem((NC, 1, LANES), F32),
            vmem((NE, 1, LANES), F32),
            vmem((plan.nz, TILE, LANES), BF16),
            vmem((TILE, LANES), F32),
            vmem((2, NE, TILE, LANES), BF16),
            dma((10,)),
            dma((NE,)),
            dma((NE,)),
            dma((NE,)),
            dma((NE,)),
            dma((NC,)),
            dma((NC,)),
            dma((NE,)),
            dma((NE,)),
            dma,
            dma,
            dma((NE,)),
            dma((NE,)),
            dma((plan.nz,)),
            dma((plan.nz,)),
            dma((NE,)),
            dma((NE,)),
            dma,
            dma,
        ],
        compiler_params=pltpu.CompilerParams(
            collective_id=0, has_side_effects=True, vmem_limit_bytes=48 * 1024 * 1024
        ),
        cost_estimate=pl.CostEstimate(
            flops=6 * NE * 9 * width * hidden,
            bytes_accessed=6 * width * hidden,
            transcendentals=NE * 9 * hidden,
        ),
    )(
        *(
            pltpu.with_memory_space_constraint(operand, pltpu.HBM)
            for operand in (
                tokens,
                routes.T,
                returns.reshape(1, count),
                router_weight.T,
                gate_weight,
                up_weight,
                down_weight,
                norm_gain,
                value_weight,
            )
        )
    )
    return values.reshape(count), grad.T


def solution(mesh):
    return jax.shard_map(
        functools.partial(on_device, mesh),
        mesh=mesh,
        in_specs=(
            P(("dp", "expert"), None),
            P(("dp", "expert"), None),
            P(("dp", "expert")),
            P(),
            P("expert", None, "tensor"),
            P("expert", None, "tensor"),
            P("expert", "tensor", None),
            P(),
            P(),
        ),
        out_specs=(P(("dp", "expert")), P()),
        check_vma=False,
    )
```

```python
import functools
import jax
import jax.numpy as jnp
from jax import lax
from jax.experimental import pallas as pl
from jax.experimental.pallas import tpu as pltpu
from jax.sharding import PartitionSpec as P

MESH = pl.DeviceIdType.MESH
F32 = jnp.float32
BF16 = jnp.bfloat16
eps = 1e-06
route_scale = 2.5
LANES = 128
EIGHT = 8
TILE = 16


class Plan:
    def __init__(self, mesh, tokens, width, hidden):
        self.nz, self.groups = mesh.shape["dp"], mesh.shape["expert"]
        self.ny = 8 if self.groups >= 32 else 2
        self.nx = self.groups // self.ny
        self.steps = ((0, 4), (2, 6), (3, 5), (1, 7)) if self.ny == 8 else ((0,), (1,))
        self.chunks = len(self.steps)
        self.joined = ((0, 1, 2), (3,)) if self.chunks == 4 else ((0, 1),)
        self.home = [one[0] for one in self.steps].index(0)
        self.each = self.groups // self.chunks
        self.tokens, self.width, self.hidden = tokens, width, hidden
        self.half = width // 2
        self.quarter = width // 4
        self.pieces = self.half // LANES
        self.packed = self.quarter + LANES
        self.main = self.each * EIGHT
        self.rows = self.main + max(TILE, self.each)


def expert_kernel(
    plan,
    tok_hbm,
    routes_hbm,
    returns_hbm,
    router_hbm,
    gate_hbm,
    up_hbm,
    down_hbm,
    gain_hbm,
    head_hbm,
    values_ref,
    grad_ref,
    tok_ref,
    routes_ref,
    returns_ref,
    router_ref,
    gain_ref,
    head_ref,
    gained_ref,
    wg,
    wu,
    wd,
    out,
    arr,
    oth,
    xs,
    pxo,
    pxi,
    ret,
    back,
    qs,
    joined,
    answer,
    mix,
    nine,
    tmp9,
    wide9,
    chosen_ref,
    sums_out,
    sums_in,
    dlo,
    dli,
    zb,
    row9,
    agb,
    w_sem,
    out_s,
    out_r,
    fwd_s,
    fwd_r,
    px_s,
    px_r,
    ret_s,
    ret_r,
    sum_s,
    sum_r,
    dl_s,
    dl_r,
    z_s,
    z_r,
    ag_s,
    ag_r,
    agx_s,
    agx_r,
):
    T, D, H, Q4 = plan.tokens, plan.width, plan.half, plan.quarter
    NZ, NE, NX, NY = plan.nz, plan.groups, plan.nx, plan.ny
    NC, CD, MAIN, XR = plan.chunks, plan.each, plan.main, plan.rows
    z = lax.axis_index("dp")
    me = lax.axis_index("expert")
    c = lax.axis_index("tensor")
    other = 1 - c
    own = plan.home * plan.each
    mx, my = lax.div(me, NY), lax.rem(me, NY)

    def hops(j, i):
        dx, b = lax.rem(i, NX), lax.div(i, NX)
        first = plan.steps[j][0]
        return dx, (first + b * (plan.steps[j][1] - first) if len(plan.steps[j]) > 1 else first)

    def ahead(j, i):
        dx, dy = hops(j, i)
        return lax.rem(mx + dx, NX) * NY + lax.rem(my + dy, NY)

    def behind(j, i):
        dx, dy = hops(j, i)
        return lax.rem(mx - dx + NX, NX) * NY + lax.rem(my - dy + NY, NY)

    def partners(j, body):
        def run(i, carry):
            body(jnp.int32(j * CD) + i, i)
            return carry

        lax.fori_loop(1 if j == plan.home else 0, CD, run, 0)

    def load(source, target, n):
        return pltpu.make_async_copy(source, target, w_sem.at[n])

    barrier = pltpu.get_barrier_semaphore()
    def greet(dz, carry):
        pl.semaphore_signal(
            barrier, inc=1, device_id=(lax.rem(z + dz, NZ), me, c), device_id_type=MESH
        )
        return carry

    lax.fori_loop(1, NZ, greet, 0)

    for j in range(NC):
        partners(
            j,
            lambda d, i, j=j: pl.semaphore_signal(
                barrier, inc=1, device_id=(z, ahead(j, i), c), device_id_type=MESH
            ),
        )
    pl.semaphore_signal(barrier, inc=1, device_id=(z, me, other), device_id_type=MESH)

    route_load = load(routes_hbm, routes_ref, 0)
    route_load.start()
    token_load = load(tok_hbm, tok_ref, 1)
    token_load.start()

    small_loads = [
        load(router_hbm, router_ref, 2),
        load(returns_hbm, returns_ref, 3),
        load(gain_hbm, gain_ref, 4),
        load(head_hbm, head_ref, 5),
    ]
    weight_loads = [
        load(gate_hbm.at[0], wg, 6),
        load(up_hbm.at[0], wu, 7),
        load(down_hbm.at[0, :, pl.ds(0, H)], wd.at[0], 8),
        load(down_hbm.at[0, :, pl.ds(H, H)], wd.at[1], 9),
    ]
    for one in small_loads + weight_loads:
        one.start()

    def out_copy(j, d, i):
        return pltpu.make_async_remote_copy(
            out.at[d], arr.at[d], out_s.at[d], out_r.at[d], (z, ahead(j, i), c), MESH
        )

    def fwd_copy(d):
        return pltpu.make_async_remote_copy(
            arr.at[d], oth.at[d], fwd_s.at[d], fwd_r.at[d], (z, me, other), MESH
        )

    def px_copy(j):
        part = pl.ds(j * CD, CD)
        return pltpu.make_async_remote_copy(
            pxo.at[part], pxi.at[part], px_s.at[j], px_r.at[j], (z, me, other), MESH
        )

    def ret_copy(j, d, i):
        return pltpu.make_async_remote_copy(
            ret.at[d], back.at[d], ret_s.at[d], ret_r.at[d], (z, behind(j, i), c), MESH
        )

    def dl_copy(j, d, i):
        return pltpu.make_async_remote_copy(
            dlo.at[j], dli.at[d], dl_s.at[d], dl_r.at[d], (z, ahead(j, i), c), MESH
        )

    def partner_of(l):
        return jnp.where(l < MAIN, lax.shift_right_logical(l, 3), l - MAIN)

    def slot_of(l):
        slot = jnp.where(l < MAIN, jnp.bitwise_and(l, 7) + 1, EIGHT + 1)
        return jnp.where(l < MAIN + CD, slot, -1).astype(F32)

    def expert_of(l, j):
        i = partner_of(l)
        b = lax.shift_right_logical(i, NX.bit_length() - 1)
        dy = jnp.full(l.shape, plan.steps[j][0], jnp.int32)
        for n in range(1, len(plan.steps[j])):
            dy = jnp.where(b == n, plan.steps[j][n], dy)
        ex = jnp.bitwise_and(mx + jnp.bitwise_and(i, NX - 1), NX - 1)
        return ex * NY + jnp.bitwise_and(my + dy, NY - 1)

    lane = lax.broadcasted_iota(jnp.int32, (1, LANES), 1)
    lane_i, lane_slot = partner_of(lane), slot_of(lane)

    def pack(dst, j, rows):
        part = pl.ds(j * CD, CD)
        first = rows[0:MAIN, 0:Q4].reshape(CD, EIGHT, Q4)
        second = rows[0:MAIN, Q4:H].reshape(CD, EIGHT, Q4)
        dst[part, :, 0:Q4] = jnp.concatenate([first, second], axis=1).astype(BF16)
        for q in range(plan.pieces):
            nine[pl.ds(q, CD, stride=TILE), :] = rows[MAIN : MAIN + CD, q * LANES : (q + 1) * LANES]
        dst[part, :, Q4:] = nine[...].reshape(CD, TILE, LANES).astype(BF16)

    def unpack(src, j, put):
        part = pl.ds(j * CD, CD)
        both = src[part, :, 0:Q4].astype(F32)
        put(0, MAIN, 0, Q4, both[:, 0:EIGHT].reshape(MAIN, Q4).astype(BF16))
        put(0, MAIN, Q4, Q4, both[:, EIGHT:TILE].reshape(MAIN, Q4).astype(BF16))
        tmp9[...] = src[part, :, Q4:].astype(F32).reshape(CD * TILE, LANES)
        last = jnp.concatenate(
            [tmp9[pl.ds(q, CD, stride=TILE), :] for q in range(plan.pieces)], axis=1
        )
        last = jnp.concatenate([last, jnp.zeros((XR - MAIN - CD, H), F32)], axis=0)
        put(MAIN, XR - MAIN, 0, H, last.astype(BF16))

    nine[...] = jnp.zeros_like(nine)
    expert_row = lax.broadcasted_iota(jnp.int32, (NE, T), 0)
    before = (
        lax.broadcasted_iota(jnp.int32, (T, T), 0) < lax.broadcasted_iota(jnp.int32, (T, T), 1)
    ).astype(BF16)
    slot_row = lax.broadcasted_iota(jnp.int32, (XR, NE), 0)
    expert_column = lax.broadcasted_iota(jnp.int32, (XR, NE), 1)
    row_slot = slot_of(lax.broadcasted_iota(jnp.int32, (XR, T), 0))
    spreads = [(expert_column == expert_of(slot_row, j)).astype(BF16) for j in range(NC)]
    route_load.wait()
    named = (expert_row == routes_ref[0:1, :]) | (expert_row == routes_ref[1:2, :])
    named = named.astype(F32)
    earlier = jnp.dot(named.astype(BF16), before, preferred_element_type=F32)
    key = (named * (earlier + 1.0)).astype(BF16)
    picks = []
    for j in range(NC):
        spread = jnp.dot(spreads[j], key, preferred_element_type=F32)
        picks.append((spread == row_slot).astype(BF16))

    columns = pl.ds(pl.multiple_of(c * H, LANES), H)
    token_load.wait()
    for j in range(NC):
        pack(out, j, jnp.dot(picks[j], tok_ref[:, columns], preferred_element_type=F32))
        if j == 0:
            pl.semaphore_wait(barrier, NE - 1 + NZ - 1 + 1)
        partners(j, lambda d, i, j=j: out_copy(j, d, i).start())
        if j == plan.home:
            arr[own] = out[own]
            fwd_copy(own).start()

    marks = [
        jnp.transpose(
            (
                lax.broadcasted_iota(jnp.int32, (LANES, T), 0) == routes_ref[k : k + 1, :]
            ).astype(F32)
        )
        for k in range(2)
    ]
    after = (
        lax.broadcasted_iota(jnp.int32, (T, T), 0) > lax.broadcasted_iota(jnp.int32, (T, T), 1)
    ).astype(BF16)
    cum = jnp.dot(after, (marks[0] + marks[1]).astype(BF16), preferred_element_type=F32)
    key = jnp.concatenate([marks[0] * (cum + 1.0), marks[1] * (cum + 1.0)], axis=0).astype(BF16)
    places = []
    for j in range(NC):
        spread = (lax.broadcasted_iota(jnp.int32, (LANES, LANES), 0) == expert_of(lane, j)).astype(
            BF16
        )
        spread = jnp.dot(key, spread, preferred_element_type=F32)
        place = (spread == lane_slot).astype(F32)
        qs[j] = place.astype(BF16)
        places.append(place[:, 0:XR])
    for n, steps in enumerate(plan.joined):
        place = jnp.concatenate([places[j] for j in steps], axis=1)
        joined[n, :, 0 : len(steps) * XR] = place.astype(BF16)

    for one in small_loads:
        one.wait()
    for n in range(0, D, 2 * LANES):
        gained = gain_ref[n : n + 2 * LANES] * head_ref[n : n + 2 * LANES].astype(F32)
        gained_ref[:, n : n + 2 * LANES] = gained.reshape(1, 2 * LANES)
    logits = lax.dot_general(
        tok_ref[...], router_ref[...], (((1,), (1,)), ((), ())), preferred_element_type=F32
    )
    scores = jax.nn.sigmoid(logits)
    for k in range(2):
        chosen = jnp.sum(marks[k][:, 0:NE] * scores, axis=1, keepdims=True)
        chosen_ref[k] = jnp.broadcast_to(chosen, (T, LANES))

    for one in weight_loads:
        one.wait()

    for j in range(NC):

        def arrive(d, i, j=j):
            out_copy(j, d, i).wait_recv()
            fwd_copy(d).start()

        partners(j, arrive)

        def put_own(r, n, col, m, v, j=j):
            xs[j, c, r : r + n, col : col + m] = v

        def put_other(r, n, col, m, v, j=j):
            xs[j, other, r : r + n, col : col + m] = v

        unpack(arr, j, put_own)

        def forwarded(i, carry, j=j):
            fwd_copy(jnp.int32(j * CD) + i).wait_recv()
            return carry

        lax.fori_loop(0, CD, forwarded, 0)
        unpack(oth, j, put_other)
        gate = jnp.dot(xs[j, 0], wg[0:H, :], preferred_element_type=F32)
        gate = gate + jnp.dot(xs[j, 1], wg[H:D, :], preferred_element_type=F32)
        upward = jnp.dot(xs[j, 0], wu[0:H, :], preferred_element_type=F32)
        upward = upward + jnp.dot(xs[j, 1], wu[H:D, :], preferred_element_type=F32)
        hidden = (gate / (1.0 + jnp.exp(-gate)) * upward).astype(BF16)
        pack(pxo, j, jnp.dot(hidden, wd[other], preferred_element_type=F32))
        px_copy(j).start()
        pack(ret, j, jnp.dot(hidden, wd[c], preferred_element_type=F32))
        px_copy(j).wait_recv()
        part = pl.ds(j * CD, CD)
        ret[part] = (ret[part].astype(F32) + pxi[part].astype(F32)).astype(BF16)
        if j == plan.home:
            back[own] = ret[own]
        partners(j, lambda d, i, j=j: ret_copy(j, d, i).start())

    for j in range(NC):
        px_copy(j).wait_send()
        partners(j, lambda d, i, j=j: out_copy(j, d, i).wait_send())

    def left_chip(d, carry):
        fwd_copy(d).wait_send()
        return carry

    lax.fori_loop(0, NE, left_chip, 0)

    for n, steps in enumerate(plan.joined):
        for k, j in enumerate(steps):

            def put_answer(r, rows, col, m, v, first=k * XR):
                answer[first + r : first + r + rows, col : col + m] = v

            partners(j, lambda d, i, j=j: ret_copy(j, d, i).wait_recv())
            unpack(back, j, put_answer)
        deep = len(steps) * XR
        term = jnp.dot(joined[n, :, 0:deep], answer[0:deep], preferred_element_type=F32)
        if n == 0:
            mix[...] = term
        else:
            mix[...] += term

    block = min(32, T)
    for b in range(T // block):
        low, high = b * block, (b + 1) * block
        first, second = chosen_ref[0, low:high], chosen_ref[1, low:high]
        total = first + second
        w0, w1 = first / total, second / total
        acc = [jnp.zeros((block, LANES), F32) for _ in range(6)]
        for q in range(plan.pieces):
            at = pl.ds(pl.multiple_of(c * H + q * LANES, LANES), LANES)
            gained = gained_ref[:, at]
            o0 = mix[low:high, q * LANES : (q + 1) * LANES]
            o1 = mix[T + low : T + high, q * LANES : (q + 1) * LANES]
            residual = tok_ref[low:high, at].astype(F32) + route_scale * (w0 * o0 + w1 * o1)
            terms = (
                residual * residual,
                residual * gained,
                residual * o0,
                residual * o1,
                gained * o0,
                gained * o1,
            )
            acc = [a + term for a, term in zip(acc, terms)]
        line = jnp.zeros((block, LANES), F32)
        for n, a in enumerate(acc):
            line = jnp.where(lane == n, jnp.sum(a, axis=1, keepdims=True), line)
        sums_out[low:high, :] = line

    sums_copy = pltpu.make_async_remote_copy(
        sums_out, sums_in, sum_s, sum_r, (z, me, other), MESH
    )
    sums_copy.start()
    raw = jnp.transpose(jnp.broadcast_to(returns_ref[...], (LANES, T)))[:, 0:1]
    sign = jnp.where(raw > 0.0, 1.0, jnp.where(raw < 0.0, -1.0, 0.0))
    target = sign * (jnp.sqrt(jnp.abs(raw) + 1.0) - 1.0) + 0.001 * raw
    first, second = chosen_ref[0][:, 0:1], chosen_ref[1][:, 0:1]
    score_sum = first + second
    w0, w1 = first / score_sum, second / score_sum
    sums_copy.wait_recv()
    sums = sums_out[...] + sums_in[...]
    rr, rg, ro0, ro1, go0, go1 = [sums[:, n : n + 1] for n in range(6)]
    inverse = lax.rsqrt(rr * (1.0 / D) + eps)
    values = rg * inverse
    error = values - target
    pull = inverse * inverse * inverse * (error * rg * (1.0 / D))
    gw0 = route_scale * (inverse * error * go0 - pull * ro0)
    gw1 = route_scale * (inverse * error * go1 - pull * ro1)
    centre = w0 * gw0 + w1 * gw1
    gl0 = (gw0 - centre) / score_sum * first * (1.0 - first)
    gl1 = (gw1 - centre) / score_sum * second * (1.0 - second)
    both = jnp.concatenate([gl0, gl1], axis=0).astype(BF16).astype(F32)

    for j in range(NC):
        dlo[j] = jnp.sum(qs[j].astype(F32) * both, axis=0, keepdims=True)
        if j == plan.home:
            dli[own] = dlo[j]
        partners(j, lambda d, i, j=j: dl_copy(j, d, i).start())

    values_ref[...] = jnp.transpose(jnp.broadcast_to(values, (T, LANES)))[0:1, :]
    sums_copy.wait_send()
    for j in range(NC):
        partners(j, lambda d, i, j=j: ret_copy(j, d, i).wait_send())

    grad = jnp.zeros((1, H), F32)
    for j in range(NC):
        partners(j, lambda d, i, j=j: dl_copy(j, d, i).wait_recv())
        got = dli[j * CD : (j + 1) * CD]
        mine = lax.broadcasted_iota(jnp.int32, (CD, 1, LANES), 0) == lane_i.reshape(1, 1, LANES)
        line = jnp.sum(jnp.where(mine, got, 0.0), axis=0)
        line = jnp.broadcast_to(line, (TILE, LANES)).astype(BF16)[:, 0:XR]
        grad = grad + jnp.dot(line, xs[j, c], preferred_element_type=F32)[0:1]

    row9[...] = jnp.zeros_like(row9)
    for q in range(plan.pieces):
        row9[q : q + 1, :] = grad[:, q * LANES : (q + 1) * LANES]
    zb[z] = row9[...].astype(BF16)

    def z_copy(n):
        dz = lax.rem(n + NZ // 2 - 1, NZ - 1) + 1
        return pltpu.make_async_remote_copy(
            zb.at[z], zb.at[z], z_s.at[n], z_r.at[z], (lax.rem(z + dz, NZ), me, c), MESH
        )

    def z_from(dz):
        source = lax.rem(z - dz + NZ, NZ)
        return pltpu.make_async_remote_copy(
            zb.at[source], zb.at[source], z_s.at[dz], z_r.at[source], (source, me, c), MESH
        )

    def z_start(dz, carry):
        z_copy(dz).start()
        return carry

    def z_wait(dz, carry):
        z_from(dz).wait_recv()
        return carry

    lax.fori_loop(1, NZ, z_start, 0)
    for j in range(NC):
        partners(j, lambda d, i, j=j: dl_copy(j, d, i).wait_send())
    lax.fori_loop(1, NZ, z_wait, 0)
    grad = zb[0].astype(F32)
    for source in range(1, NZ):
        grad = grad + zb[source].astype(F32)

    agb[c, me] = grad.astype(BF16)

    def ag_copy(j, d, i):
        return pltpu.make_async_remote_copy(
            agb.at[c, me], agb.at[c, me], ag_s.at[d], ag_r.at[d], (z, ahead(j, i), c), MESH
        )

    def ag_from(j, d, i):
        source = behind(j, i)
        return pltpu.make_async_remote_copy(
            agb.at[c, source], agb.at[c, source], ag_s.at[d], ag_r.at[d], (z, source, c), MESH
        )

    for j in range(NC):
        partners(j, lambda d, i, j=j: ag_copy(j, d, i).start())

    def left_plane(dz, carry):
        z_copy(dz).wait_send()
        return carry

    lax.fori_loop(1, NZ, left_plane, 0)
    for j in range(NC):
        partners(j, lambda d, i, j=j: ag_from(j, d, i).wait_recv())
    agx = pltpu.make_async_remote_copy(
        agb.at[c], agb.at[c], agx_s, agx_r, (z, me, other), MESH
    )
    agx.start()

    def write(part):
        wide9[...] = agb[part].astype(F32).reshape(NE * TILE, LANES)
        for q in range(plan.pieces):
            at = pl.ds(pl.multiple_of(part * H + q * LANES, LANES), LANES)
            grad_ref[:, at] = wide9[pl.ds(q, NE, stride=TILE), :].astype(BF16)

    write(c)
    for j in range(NC):
        partners(j, lambda d, i, j=j: ag_copy(j, d, i).wait_send())
    agx.wait()
    write(other)


def on_device(
    mesh,
    tokens,
    routes,
    returns,
    router_weight,
    gate_weight,
    up_weight,
    down_weight,
    norm_gain,
    value_weight,
):
    count, width = tokens.shape
    hidden = gate_weight.shape[2]
    plan = Plan(mesh, count, width, hidden)
    NE, NC, H = plan.groups, plan.chunks, plan.half
    packed = (NE, TILE, plan.packed)
    vmem, dma = pltpu.VMEM, pltpu.SemaphoreType.DMA
    in_place = pl.BlockSpec(memory_space=pl.ANY)
    values, grad = pl.pallas_call(
        functools.partial(expert_kernel, plan),
        out_shape=(
            jax.ShapeDtypeStruct((1, count), F32),
            jax.ShapeDtypeStruct((NE, width), BF16),
        ),
        in_specs=[in_place] * 9,
        out_specs=(pl.BlockSpec(memory_space=pltpu.VMEM),) * 2,
        scratch_shapes=[
            vmem((count, width), BF16),
            vmem((2, count), jnp.int32),
            vmem((1, count), F32),
            vmem((NE, width), BF16),
            vmem((width,), F32),
            vmem((width,), BF16),
            vmem((1, width), F32),
            vmem((width, hidden), BF16),
            vmem((width, hidden), BF16),
            vmem((2, hidden, H), BF16),
            vmem(packed, BF16),
            vmem(packed, BF16),
            vmem(packed, BF16),
            vmem((NC, 2, plan.rows, H), BF16),
            vmem(packed, BF16),
            vmem(packed, BF16),
            vmem(packed, BF16),
            vmem(packed, BF16),
            vmem((NC, 2 * count, LANES), BF16),
            vmem((len(plan.joined), 2 * count, 2 * LANES), BF16),
            vmem((max(map(len, plan.joined)) * plan.rows, H), BF16),
            vmem((2 * count, H), F32),
            vmem((plan.each * TILE, LANES), F32),
            vmem((plan.each * TILE, LANES), F32),
            vmem((NE * TILE, LANES), F32),
            vmem((2, count, LANES), F32),
            vmem((count, LANES), F32),
            vmem((count, LANES), F32),
            vmem((NC, 1, LANES), F32),
            vmem((NE, 1, LANES), F32),
            vmem((plan.nz, TILE, LANES), BF16),
            vmem((TILE, LANES), F32),
            vmem((2, NE, TILE, LANES), BF16),
            dma((10,)),
            dma((NE,)),
            dma((NE,)),
            dma((NE,)),
            dma((NE,)),
            dma((NC,)),
            dma((NC,)),
            dma((NE,)),
            dma((NE,)),
            dma,
            dma,
            dma((NE,)),
            dma((NE,)),
            dma((plan.nz,)),
            dma((plan.nz,)),
            dma((NE,)),
            dma((NE,)),
            dma,
            dma,
        ],
        compiler_params=pltpu.CompilerParams(
            collective_id=0, has_side_effects=True, vmem_limit_bytes=48 * 1024 * 1024
        ),
        cost_estimate=pl.CostEstimate(
            flops=6 * NE * 9 * width * hidden,
            bytes_accessed=6 * width * hidden,
            transcendentals=NE * 9 * hidden,
        ),
    )(
        *(
            pltpu.with_memory_space_constraint(operand, pltpu.HBM)
            for operand in (
                tokens,
                routes.T,
                returns.reshape(1, count),
                router_weight.T,
                gate_weight,
                up_weight,
                down_weight,
                norm_gain,
                value_weight,
            )
        )
    )
    return values.reshape(count), grad.T


def solution(mesh):
    return jax.shard_map(
        functools.partial(on_device, mesh),
        mesh=mesh,
        in_specs=(
            P(("dp", "expert"), None),
            P(("dp", "expert"), None),
            P(("dp", "expert")),
            P(),
            P("expert", None, "tensor"),
            P("expert", None, "tensor"),
            P("expert", "tensor", None),
            P(),
            P(),
        ),
        out_specs=(P(("dp", "expert")), P()),
        check_vma=False,
    )
```
